32 devices in a mesh: row: 4 (over x, core), col: 8 (over z, y).
Axes of the slice: x: 2, y: 2, z: 4, core: 2. Of those that a mesh axis runs over, the one named last changes fastest.
Arguments:
- homolog_embedding: bfloat16 [128, 32, 64], P(None, ('row', 'col')), may hold values from -6 to 6
- standardize_factor: float32 [64], replicated, may hold values from 0.5 to 1.5
- standardize_shift: float32 [64], replicated, may hold values from -3 to 3
- mapping_matrix: bfloat16 [64, 64], replicated, may hold values from -0.75 to 0.75
- output_weight: bfloat16 [1024, 128], replicated, may hold values from -0.1875 to 0.1875
- output_bias: float32 [128], replicated, may hold values from -3 to 3
- cotangent: bfloat16 [32, 32, 128], P('row', 'col'), may hold values from -0.59765625 to 0.59765625
Outputs:
- pair_update_output: bfloat16 [32, 32, 128], P('row', 'col')
- alignment_gradient: float32 [128, 32, 64], P(None, ('row', 'col'))
- projection_gradient: float32 [64, 64], replicated
- output_weight_gradient: float32 [1024, 128], replicated
- norm_gain_gradient: float32 [64], replicated
- norm_bias_gradient: float32 [64], replicated
The draws below stay inside these ranges and needn't reach their ends.
All inputs are finite; a program needn't handle non-finite values.
Results may differ from the reference program's by a relative error of at most 0.0075.
Values may be sent and summed in bfloat16 or wider, within the bound.
A program may use at most 64 MiB of HBM per device.

```python
import jax
import jax.numpy as jnp
from jax import lax

EMBED_FEATURE_DIM = 64
FACTOR_DIM = 32
DUAL_EMBED_DIM = 128
HOMOLOG_NUMBER = 128
RES_DEV = 1
WINDOW_POSITIONS = 32
N_ROW = 4


def block_levels(own_key, shape, pieces, least, high):
    loudness, own = 1.0, jax.random.fold_in(own_key, 6)
    for axis_at, shards_of in pieces:
        draws = jnp.exp(jax.random.uniform(jax.random.fold_in(own, axis_at), (shards_of,), jnp.float32, least / len(pieces), high / len(pieces)))
        loudness = loudness * jnp.repeat(draws, shape[axis_at] // shards_of).reshape([-1 if axis == axis_at else 1 for axis in range(len(shape))])
    return loudness


def scatter_about(own_key, extent, width, most, shards=(), kind=jnp.bfloat16):
    array = jax.random.normal(own_key, extent, jnp.float32) * width
    if len(shards) > 0:
        array = block_levels(own_key, extent, shards, -0.22, 0.18) * array
    return jnp.clip(array, min=-most, max=most).astype(kind)


def setup_inputs(seed: int = 0) -> dict:
    keys = jax.random.split(jax.random.key(seed), 8)
    homolog_embedding = scatter_about(keys[0], (HOMOLOG_NUMBER, WINDOW_POSITIONS, EMBED_FEATURE_DIM), 1.0, 6.0, ((1, 32),))
    standardize_factor = jnp.clip(1.0 + 0.1 * jax.random.normal(keys[1], (EMBED_FEATURE_DIM,), jnp.float32), 0.5, 1.5)
    standardize_shift = scatter_about(keys[2], (EMBED_FEATURE_DIM,), 0.5, 3.0, (), jnp.float32)
    mapping_matrix = scatter_about(keys[3], (EMBED_FEATURE_DIM, 2 * FACTOR_DIM), EMBED_FEATURE_DIM ** -0.5, 0.75)
    output_weight = scatter_about(keys[4], (FACTOR_DIM * FACTOR_DIM, DUAL_EMBED_DIM), (FACTOR_DIM * FACTOR_DIM) ** -0.5, 0.1875)
    output_bias = scatter_about(keys[5], (DUAL_EMBED_DIM,), 0.5, 3.0, (), jnp.float32)
    cotangent = scatter_about(keys[6], (WINDOW_POSITIONS, WINDOW_POSITIONS, DUAL_EMBED_DIM), 0.1, 0.59765625, ((0, 4), (1, 8)))
    return dict(homolog_embedding=homolog_embedding, standardize_factor=standardize_factor, standardize_shift=standardize_shift, mapping_matrix=mapping_matrix, output_weight=output_weight, output_bias=output_bias, cotangent=cotangent)


def normalized_rows(values, standardize_factor, standardize_shift):
    values = values.astype(jnp.float32)
    mean_row = lax.optimization_barrier(jnp.mean(values, axis=-1, keepdims=True))
    centred = values - mean_row
    variance = lax.optimization_barrier(jnp.mean(centred * centred, axis=-1, keepdims=True))
    reciprocal_scale = lax.rsqrt(variance + 1e-05)
    single_unit_rows = centred * reciprocal_scale
    return (single_unit_rows * standardize_factor + standardize_shift, single_unit_rows, reciprocal_scale)

def reference(homolog_embedding, standardize_factor, standardize_shift, mapping_matrix, output_weight, output_bias, cotangent):
    normalized_complete, single_unit_rows, reciprocal_scale = normalized_rows(homolog_embedding, standardize_factor, standardize_shift)
    normed = normalized_complete.astype(jnp.bfloat16)
    proj = jnp.einsum('snm,mk->snk', normed.astype(jnp.float32), mapping_matrix.astype(jnp.float32)).astype(jnp.bfloat16)
    left_band = proj[..., :FACTOR_DIM].astype(jnp.float32)
    latter_vertical_band = proj[..., FACTOR_DIM:].astype(jnp.float32)
    block_rows = RES_DEV * N_ROW
    block_count = WINDOW_POSITIONS // block_rows
    weight_f = output_weight.astype(jnp.float32)

    def one_block(carry, block_index):
        weight_acc, latter_running_total = carry
        first_row = (block_index * block_rows).astype(jnp.int32)
        former_tile_piece = lax.dynamic_slice_in_dim(left_band, first_row, block_rows, 1)
        grad_blk = lax.dynamic_slice_in_dim(cotangent, first_row, block_rows, 0).astype(jnp.float32)
        tensor_product_tile = (jnp.einsum('ejt,ecd->jctd', former_tile_piece, latter_vertical_band) / HOMOLOG_NUMBER).astype(jnp.bfloat16)
        tensor_product_tile = tensor_product_tile.reshape(block_rows, WINDOW_POSITIONS, FACTOR_DIM * FACTOR_DIM).astype(jnp.float32)
        pair_blk = (jnp.einsum('ijk,ke->ije', tensor_product_tile, weight_f) + output_bias).astype(jnp.bfloat16)
        grad_outer = jnp.einsum('ije,ke->ijk', grad_blk, weight_f).astype(jnp.bfloat16).astype(jnp.float32)
        weight_acc = weight_acc + jnp.einsum('ijk,ije->ke', tensor_product_tile, grad_blk)
        quadruple_cotangent = grad_outer.reshape(block_rows, WINDOW_POSITIONS, FACTOR_DIM, FACTOR_DIM)
        former_factor_cotangent = jnp.einsum('lcaz,ycz->yla', quadruple_cotangent, latter_vertical_band) / HOMOLOG_NUMBER
        latter_running_total = latter_running_total + jnp.einsum('wqcp,nwc->nqp', quadruple_cotangent, former_tile_piece) / HOMOLOG_NUMBER
        return ((weight_acc, latter_running_total), (pair_blk, former_factor_cotangent))
    starting_state = (jnp.zeros((FACTOR_DIM * FACTOR_DIM, DUAL_EMBED_DIM), jnp.float32), jnp.zeros((HOMOLOG_NUMBER, WINDOW_POSITIONS, FACTOR_DIM), jnp.float32))
    (output_weight_gradient, right_grad), (pair_blocks, former_tile_sequence) = lax.scan(one_block, starting_state, jnp.arange(block_count, dtype=jnp.int32))
    pair_update_output = pair_blocks.reshape(WINDOW_POSITIONS, WINDOW_POSITIONS, DUAL_EMBED_DIM)
    former_factor_cotangent = jnp.transpose(former_tile_sequence, (1, 0, 2, 3)).reshape(HOMOLOG_NUMBER, WINDOW_POSITIONS, FACTOR_DIM)
    grad_act = jnp.concatenate([former_factor_cotangent, right_grad], axis=-1).astype(jnp.bfloat16).astype(jnp.float32)
    projection_gradient = jnp.einsum('snm,snk->mk', normed.astype(jnp.float32), grad_act)
    grad_normed = jnp.einsum('snk,mk->snm', grad_act, mapping_matrix.astype(jnp.float32))
    norm_gain_gradient = lax.optimization_barrier(jnp.sum(grad_normed * single_unit_rows, axis=(0, 1)))
    norm_bias_gradient = lax.optimization_barrier(jnp.sum(grad_normed, axis=(0, 1)))
    rescaled_values = grad_normed * standardize_factor
    alignment_gradient = reciprocal_scale * (rescaled_values - lax.optimization_barrier(jnp.mean(rescaled_values, axis=-1, keepdims=True)) - single_unit_rows * lax.optimization_barrier(jnp.mean(rescaled_values * single_unit_rows, axis=-1, keepdims=True)))
    return (pair_update_output, alignment_gradient, projection_gradient, output_weight_gradient, norm_gain_gradient, norm_bias_gradient)
```

```python
import functools

import jax
import jax.numpy as jnp
from jax import lax
from jax.experimental import pallas as pl
from jax.experimental.pallas import tpu as pltpu
from jax.sharding import PartitionSpec as P

F32, BF16 = jnp.float32, jnp.bfloat16
MESH = pl.DeviceIdType.MESH


def swap_blocks(parts, width):
    axis = parts[0].ndim - 1
    lane = lax.broadcasted_iota(jnp.int32, parts[0].shape, axis)
    a0, a1, a2, a3 = parts
    total = 4 * width
    half = lane < 2 * width
    t0 = jnp.where(half, a0, pltpu.roll(a2, 2 * width, axis))
    t2 = jnp.where(half, pltpu.roll(a0, 2 * width, axis), a2)
    t1 = jnp.where(half, a1, pltpu.roll(a3, 2 * width, axis))
    t3 = jnp.where(half, pltpu.roll(a1, 2 * width, axis), a3)
    even = lane % (2 * width) < width
    u0 = jnp.where(even, t0, pltpu.roll(t1, width, axis))
    u1 = jnp.where(even, pltpu.roll(t0, total - width, axis), t1)
    u2 = jnp.where(even, t2, pltpu.roll(t3, width, axis))
    u3 = jnp.where(even, pltpu.roll(t2, total - width, axis), t3)
    return [u0, u1, u2, u3]


def dot(a, b, ca, cb):
    return lax.dot_general(a, b, (((ca,), (cb,)), ((), ())), preferred_element_type=F32)


def kernel(
    cfg, x_ref, gain_ref, shift_ref, map_ref, w_ref, bias_ref, cot_ref,
    pair_ref, align_ref, proj_ref, wg_ref, gg_ref, bg_ref,
    xbuf, lf, cotf, pairf, glf, sl, sr, rl, rr, s1, r1, s2, r2, gbuf, ebuf,
    x_send, x_recv, e_send, e_recv, s1_send, s1_recv, s2_send, s2_recv,
    g2_send, g2_recv, g1_send, g1_recv,
):
    R, C, BR, BC, S, M, K, CH1, EX, CH2, NO = cfg
    r, c = lax.axis_index("row"), lax.axis_index("col")
    n = r * C + c
    dest_col, dest_slot = lax.div(n, BC), lax.rem(n, BC)
    self_right = dest_col == c
    inv = 1.0 / S

    def other(rr_, cc_):
        return jnp.logical_or(rr_ != r, cc_ != c)

    owners = []
    for k in range(BC):
        o = c * BC + k
        owners.append((lax.div(o, C), lax.rem(o, C)))

    def signal(dev):
        pl.semaphore_signal(barrier, inc=1, device_id=dev, device_id_type=MESH)

    def remote(src, dst, send, recv, dev):
        return pltpu.make_async_remote_copy(
            src_ref=src, dst_ref=dst, send_sem=send, recv_sem=recv, device_id=dev, device_id_type=MESH
        )

    barrier = pltpu.get_barrier_semaphore()
    for off in range(1, C):
        signal((r, lax.rem(c + off, C)))
    for off in range(1, R):
        signal((lax.rem(r + off, R), c))
    for q in range(R):
        @pl.when(other(q, dest_col))
        def _():
            signal((q, dest_col))
    for k in range(BC):
        @pl.when(other(*owners[k]))
        def _():
            signal(owners[k])

    own = jnp.transpose(x_ref[...].astype(F32))
    own16 = own.astype(BF16)
    xbuf[c] = own16

    @pl.when(self_right)
    def _():
        xbuf[BR + dest_slot] = own16

    pl.semaphore_wait(barrier, C - 1 + R - 1 + R + BC - jnp.where(self_right, 2, 0))

    pending = []
    for q in range(R):
        cp = remote(
            xbuf.at[c], xbuf.at[BR + dest_slot], x_send.at[C + q], x_recv.at[BR + dest_slot], (q, dest_col)
        )
        cond = other(q, dest_col)

        @pl.when(cond)
        def _():
            cp.start()
        pending.append((cp, cond))
    for off in range(1, C):
        q = lax.rem(c + off, C)
        cp = remote(xbuf.at[c], xbuf.at[c], x_send.at[q], x_recv.at[c], (r, q))
        cp.start()
        pending.append((cp, None))

    factor = jnp.transpose(jnp.broadcast_to(gain_ref[...], (S, M)))
    shift = jnp.transpose(jnp.broadcast_to(shift_ref[...], (S, M)))
    mapping = map_ref[...]
    mapping_t = jnp.transpose(mapping.astype(F32)).astype(BF16)
    cotf[...] = cot_ref[...].astype(F32)
    cot = jnp.concatenate([cotf[pl.ds(j, BR, stride=BC), :] for j in range(BC)], axis=0).astype(BF16)
    w = w_ref[...]
    groups = K * K // 128
    G = dot(cot, w, 1, 1).astype(BF16).astype(F32)
    tiles = []
    for t in range(BC // 4):
        parts = []
        for j in range(4):
            row = (4 * t + j) * BR
            parts.append(jnp.stack([G[row:row + BR, 128 * g:128 * g + 128] for g in range(groups)], axis=0))
        b = swap_blocks(parts, K)
        tiles.append(jnp.stack(b, axis=1).reshape(K * BR, 128))
    g2 = jnp.concatenate(tiles, axis=1).astype(BF16)

    def standardized(x):
        mean = jnp.mean(x, axis=0, keepdims=True)
        cen = x - mean
        scale = lax.rsqrt(jnp.mean(cen * cen, axis=0, keepdims=True) + 1e-05)
        return cen * scale, scale

    own_unit, own_scale = standardized(own)

    for off in range(1, C):
        q = lax.rem(c + off, C)
        remote(xbuf.at[q], xbuf.at[q], x_send.at[q], x_recv.at[q], (r, q)).wait_recv()
    for k in range(BC):
        @pl.when(other(*owners[k]))
        def _():
            remote(
                xbuf.at[BR + k], xbuf.at[BR + k], x_send.at[0], x_recv.at[BR + k], owners[k]
            ).wait_recv()

    units, normeds = [], []
    for i in range(BR + BC):
        unit, _ = standardized(xbuf[i].astype(F32))
        units.append(unit)
        normeds.append((unit * factor + shift).astype(BF16))
    normed = jnp.concatenate(normeds, axis=1)
    proj = dot(mapping_t, normed, 1, 0)
    for i in range(BR):
        lf[pl.ds(i, K, stride=BR), :] = proj[:K, S * i:S * i + S].astype(BF16).astype(F32)
    left = lf[...].astype(BF16)
    right = jnp.concatenate(
        [proj[K:, S * (BR + j):S * (BR + j) + S] for j in range(BC)], axis=0
    ).astype(BF16)
    outer = (dot(left, right, 1, 1) * inv).astype(BF16).astype(F32)
    rows = []
    for t in range(BC // 4):
        o = outer[:, 128 * t:128 * t + 128].reshape(groups, 4, BR, 128)
        b = swap_blocks([o[:, q] for q in range(4)], K)
        for j in range(4):
            rows.append(jnp.concatenate([b[j][g] for g in range(groups)], axis=1))
    ot = jnp.concatenate(rows, axis=0).astype(BF16)

    wgrad = dot(ot, cot, 0, 0).astype(BF16)
    for p in range(R):
        s1[p, :CH1, :] = wgrad[p * CH1:(p + 1) * CH1]

    glf[...] = dot(g2, right, 1, 0) * inv
    gr = (dot(g2, left, 0, 0) * inv).astype(BF16)
    gls = []
    for i in range(BR):
        gl = glf[pl.ds(i, K, stride=BR), :].astype(BF16)
        gls.append(gl)
        sl[i] = gl
    grs = []
    for j in range(BC):
        gg = gr[j * K:(j + 1) * K]
        grs.append(gg)
        sr[j] = gg
    rl[c] = sl[c]

    @pl.when(self_right)
    def _():
        rr[r] = sr[dest_slot]

    for off in range(1, C):
        q = lax.rem(c + off, C)
        cp = remote(sl.at[q], rl.at[c], e_send.at[q], e_recv.at[c], (r, q))
        cp.start()
        pending.append((cp, None))
    for k in range(BC):
        cp = remote(sr.at[k], rr.at[r], e_send.at[C + k], e_recv.at[C + r], owners[k])
        cond = other(*owners[k])

        @pl.when(cond)
        def _():
            cp.start()
        pending.append((cp, cond))

    glc = jnp.concatenate(gls, axis=1)
    grc = jnp.concatenate(grs, axis=1)
    cut = BR * S
    ebuf[...] = jnp.zeros_like(ebuf)
    ebuf[:, :K] = dot(normed[:, :cut], glc, 1, 1)
    ebuf[:, K:2 * K] = dot(normed[:, cut:], grc, 1, 1)
    gn = jnp.concatenate([dot(mapping[:, :K], glc, 1, 0), dot(mapping[:, K:], grc, 1, 0)], axis=1)
    bsum, gsum = jnp.zeros((M, S), F32), jnp.zeros((M, S), F32)
    for i in range(BR + BC):
        piece = gn[:, S * i:S * i + S]
        bsum = bsum + piece
        gsum = gsum + piece * units[i]
    ebuf[:, 2 * K:2 * K + 1] = jnp.sum(gsum, axis=1, keepdims=True)
    ebuf[:, 2 * K + 1:2 * K + 2] = jnp.sum(bsum, axis=1, keepdims=True)
    extra = ebuf[...].astype(BF16)
    for p in range(R):
        if p * EX < M:
            s1[p, CH1:, :] = extra[p * EX:(p + 1) * EX]
        else:
            s1[p, CH1:, :] = jnp.zeros((EX, 128), BF16)

    for off in range(1, R):
        p = lax.rem(r + off, R)
        cp = remote(s1.at[p], r1.at[r], s1_send.at[p], s1_recv.at[r], (p, c))
        cp.start()
        pending.append((cp, None))
    r1[r] = s1[r]
    for off in range(1, R):
        p = lax.rem(r + off, R)
        remote(s1.at[p], r1.at[p], s1_send.at[p], s1_recv.at[p], (p, c)).wait_recv()
    acc = r1[0].astype(F32)
    for p in range(1, R):
        acc = acc + r1[p].astype(F32)
    acc = acc.astype(BF16)
    for q in range(C):
        u = q % NO
        s2[q, :CH2, :] = acc[u * CH2:(u + 1) * CH2]
        s2[q, CH2:, :] = acc[CH1:]

    for off in range(1, C):
        q = lax.rem(c + off, C)
        cp = remote(s2.at[q], r2.at[c], s2_send.at[q], s2_recv.at[c], (r, q))
        cp.start()
        pending.append((cp, None))
    r2[c] = s2[c]

    for off in range(1, C):
        q = lax.rem(c + off, C)
        remote(sl.at[q], rl.at[q], e_send.at[q], e_recv.at[q], (r, q)).wait_recv()
    for q in range(R):
        @pl.when(other(q, dest_col))
        def _():
            remote(sr.at[0], rr.at[q], e_send.at[C], e_recv.at[C + q], (q, dest_col)).wait_recv()
    al = rl[0].astype(F32)
    for q in range(1, C):
        al = al + rl[q].astype(F32)
    ar = rr[0].astype(F32)
    for q in range(1, R):
        ar = ar + rr[q].astype(F32)
    act = jnp.concatenate([al, ar], axis=0).astype(BF16)
    scaled = dot(mapping, act, 1, 0) * factor
    align = own_scale * (
        scaled
        - jnp.mean(scaled, axis=0, keepdims=True)
        - own_unit * jnp.mean(scaled * own_unit, axis=0, keepdims=True)
    )
    align_ref[...] = jnp.transpose(align)
    pairs = dot(ot, w, 1, 0) + bias_ref[...]
    for j in range(BC):
        pairf[pl.ds(j, BR, stride=BC), :] = pairs[j * BR:(j + 1) * BR]
    pair_ref[...] = pairf[...].astype(BF16)

    for off in range(1, C):
        q = lax.rem(c + off, C)
        remote(s2.at[q], r2.at[q], s2_send.at[q], s2_recv.at[q], (r, q)).wait_recv()
    acc = r2[0].astype(F32)
    for q in range(1, C):
        acc = acc + r2[q].astype(F32)
    acc = acc.astype(BF16)
    gbuf[r, CH1:, :] = acc[CH2:]

    place = pl.ds(pl.multiple_of(lax.rem(c, NO) * CH2, 16), CH2)

    def spread():
        gbuf[r, place, :] = acc[:CH2]
        for off in range(1, C):
            q = lax.rem(c + off, C)
            remote(gbuf.at[r, place], gbuf.at[r, place], g2_send.at[q], g2_recv.at[c], (r, q)).start()

    def spread_done():
        for off in range(1, C):
            q = lax.rem(c + off, C)
            remote(gbuf.at[r, place], gbuf.at[r, place], g2_send.at[q], g2_recv.at[c], (r, q)).wait_send()

    if NO == C:
        spread()
    else:
        pl.when(c < NO)(spread)
    for q in range(NO):
        where = pl.ds(q * CH2, CH2)

        @pl.when(c != q)
        def _():
            remote(gbuf.at[r, where], gbuf.at[r, where], g2_send.at[q], g2_recv.at[q], (r, q)).wait_recv()
    for off in range(1, R):
        p = lax.rem(r + off, R)
        cp = remote(gbuf.at[r], gbuf.at[r], g1_send.at[p], g1_recv.at[r], (p, c))
        cp.start()
        pending.append((cp, None))
    for off in range(1, R):
        p = lax.rem(r + off, R)
        remote(gbuf.at[p], gbuf.at[p], g1_send.at[p], g1_recv.at[p], (p, c)).wait_recv()
    for p in range(R):
        wg_ref[p * CH1:(p + 1) * CH1, :] = gbuf[p, :CH1, :].astype(F32)
        if p * EX < M:
            ebuf[p * EX:(p + 1) * EX, :] = gbuf[p, CH1:, :].astype(F32)
    proj_ref[...] = ebuf[:, :2 * K]
    flipped = jnp.transpose(ebuf[...])
    gg_ref[...] = flipped[2 * K:2 * K + 1, :]
    bg_ref[...] = flipped[2 * K + 1:2 * K + 2, :]

    if NO == C:
        spread_done()
    else:
        pl.when(c < NO)(spread_done)
    for cp, cond in pending:
        if cond is None:
            cp.wait_send()
        else:
            pl.when(cond)(cp.wait_send)


def shards(x, gain, shift, mapping, w, bias, cot):
    R, C = lax.axis_size("row"), lax.axis_size("col")
    S, M = x.shape[0], x.shape[2]
    K = mapping.shape[1] // 2
    BR, BC, E = cot.shape
    rows = w.shape[0]
    CH1, EX = rows // R, max(16, M // R)
    CH2 = max(16, CH1 // C)
    NO = CH1 // CH2
    cfg = (R, C, BR, BC, S, M, K, CH1, EX, CH2, NO)
    vm = pl.BlockSpec(memory_space=pltpu.VMEM)
    sem = pltpu.SemaphoreType.DMA
    pair, align, proj, wg, gg, bg = pl.pallas_call(
        functools.partial(kernel, cfg),
        out_shape=[
            jax.ShapeDtypeStruct((BR * BC, E), BF16),
            jax.ShapeDtypeStruct((S, M), F32),
            jax.ShapeDtypeStruct((M, 2 * K), F32),
            jax.ShapeDtypeStruct((rows, E), F32),
            jax.ShapeDtypeStruct((1, M), F32),
            jax.ShapeDtypeStruct((1, M), F32),
        ],
        in_specs=[vm] * 7,
        out_specs=[vm] * 6,
        scratch_shapes=[
            pltpu.VMEM((BR + BC, M, S), BF16),
            pltpu.VMEM((K * BR, S), F32),
            pltpu.VMEM((BR * BC, E), F32),
            pltpu.VMEM((BR * BC, E), F32),
            pltpu.VMEM((K * BR, S), F32),
            pltpu.VMEM((BR, K, S), BF16),
            pltpu.VMEM((BC, K, S), BF16),
            pltpu.VMEM((C, K, S), BF16),
            pltpu.VMEM((R, K, S), BF16),
            pltpu.VMEM((R, CH1 + EX, E), BF16),
            pltpu.VMEM((R, CH1 + EX, E), BF16),
            pltpu.VMEM((C, CH2 + EX, E), BF16),
            pltpu.VMEM((C, CH2 + EX, E), BF16),
            pltpu.VMEM((R, CH1 + EX, E), BF16),
            pltpu.VMEM((M, E), F32),
            sem((C + R,)), sem((BR + BC,)),
            sem((C + BC,)), sem((C + R,)),
            sem((R,)), sem((R,)),
            sem((C,)), sem((C,)),
            sem((C,)), sem((C,)),
            sem((R,)), sem((R,)),
        ],
        compiler_params=pltpu.CompilerParams(
            collective_id=0, has_side_effects=True, vmem_limit_bytes=48 * 1024 * 1024
        ),
        name="outer_mean",
    )(
        x.reshape(S, M), gain.reshape(1, M), shift.reshape(1, M), mapping, w,
        bias.reshape(1, E), cot.reshape(BR * BC, E),
    )
    return (
        pair.reshape(BR, BC, E), align.reshape(S, 1, M), proj, wg, gg.reshape(M), bg.reshape(M)
    )


def solution(mesh):
    in_specs = (P(None, ("row", "col"), None), P(), P(), P(), P(), P(), P("row", "col", None))
    out_specs = (P("row", "col", None), P(None, ("row", "col"), None), P(), P(), P(), P())
    return jax.shard_map(shards, mesh=mesh, in_specs=in_specs, out_specs=out_specs, check_vma=False)
```

```python
import functools

import jax
import jax.numpy as jnp
from jax import lax
from jax.experimental import pallas as pl
from jax.experimental.pallas import tpu as pltpu
from jax.sharding import PartitionSpec as P

F32, BF16 = jnp.float32, jnp.bfloat16
MESH = pl.DeviceIdType.MESH


def swap_blocks(parts, width):
    axis = parts[0].ndim - 1
    lane = lax.broadcasted_iota(jnp.int32, parts[0].shape, axis)
    a0, a1, a2, a3 = parts
    total = 4 * width
    half = lane < 2 * width
    t0 = jnp.where(half, a0, pltpu.roll(a2, 2 * width, axis))
    t2 = jnp.where(half, pltpu.roll(a0, 2 * width, axis), a2)
    t1 = jnp.where(half, a1, pltpu.roll(a3, 2 * width, axis))
    t3 = jnp.where(half, pltpu.roll(a1, 2 * width, axis), a3)
    even = lane % (2 * width) < width
    u0 = jnp.where(even, t0, pltpu.roll(t1, width, axis))
    u1 = jnp.where(even, pltpu.roll(t0, total - width, axis), t1)
    u2 = jnp.where(even, t2, pltpu.roll(t3, width, axis))
    u3 = jnp.where(even, pltpu.roll(t2, total - width, axis), t3)
    return [u0, u1, u2, u3]


def dot(a, b, ca, cb):
    return lax.dot_general(a, b, (((ca,), (cb,)), ((), ())), preferred_element_type=F32)


def kernel(
    cfg, x_hbm, gain_hbm, shift_hbm, map_hbm, w_hbm, bias_hbm, cot_hbm,
    pair_ref, align_ref, gout_ref, gxout_ref,
    gain_ref, shift_ref, map_ref, w_ref, bias_ref, cot_ref,
    xbuf, lf, cotf, pairf, glf, sl, sr, rl, rr, s1, r1, s2, r2, gbuf, ebuf, s1x, r1x, r2x, gx,
    load, x_send, x_recv, e_send, e_recv, s1_send, s1_recv, s2_send, s2_recv,
    g2_send, g2_recv, g1_send, g1_recv, x1_send, x1_recv, x2_send, x2_recv, x3_send, x3_recv,
):
    R, C, BR, BC, S, M, K, CH1, EX, CH2, NO = cfg
    r, c = lax.axis_index("row"), lax.axis_index("col")
    n = r * C + c
    dest_col, dest_slot = lax.div(n, BC), lax.rem(n, BC)
    self_right = dest_col == c
    inv = 1.0 / S
    row_peers = [lax.rem(r + off, R) for off in range(1, R)]
    col_peers = [lax.rem(c + off, C) for off in range(1, C)]

    loads = [
        pltpu.make_async_copy(src, dst, load.at[i])
        for i, (src, dst) in enumerate([
            (x_hbm, xbuf.at[c]), (cot_hbm, cot_ref), (w_hbm, w_ref), (map_hbm, map_ref),
            (gain_hbm, gain_ref), (shift_hbm, shift_ref), (bias_hbm, bias_ref),
        ])
    ]
    for cp in loads:
        cp.start()

    def other(rr_, cc_):
        return jnp.logical_or(rr_ != r, cc_ != c)

    owners = []
    for k in range(BC):
        o = c * BC + k
        owners.append((lax.div(o, C), lax.rem(o, C)))

    def signal(dev):
        pl.semaphore_signal(barrier, inc=1, device_id=dev, device_id_type=MESH)

    def remote(src, dst, send, recv, dev):
        return pltpu.make_async_remote_copy(
            src_ref=src, dst_ref=dst, send_sem=send, recv_sem=recv, device_id=dev, device_id_type=MESH
        )

    def owning(q, f):
        if NO == C:
            f()
        else:
            pl.when(q < NO)(f)

    barrier = pltpu.get_barrier_semaphore()
    for q in col_peers:
        signal((r, q))
    for p in row_peers:
        signal((p, c))
    for q in range(R):
        @pl.when(other(q, dest_col))
        def _():
            signal((q, dest_col))
    for k in range(BC):
        @pl.when(other(*owners[k]))
        def _():
            signal(owners[k])

    loads[0].wait()

    @pl.when(self_right)
    def _():
        xbuf[BR + dest_slot] = xbuf[c]

    pl.semaphore_wait(barrier, C - 1 + R - 1 + R + BC - jnp.where(self_right, 2, 0))

    pending = []

    def send(src, dst, ssem, rsem, dev, cond=None):
        cp = remote(src, dst, ssem, rsem, dev)
        if cond is None:
            cp.start()
        else:
            pl.when(cond)(cp.start)
        pending.append((cp, cond))

    for q in range(R):
        send(
            xbuf.at[c], xbuf.at[BR + dest_slot], x_send.at[C + q], x_recv.at[BR + dest_slot],
            (q, dest_col), other(q, dest_col),
        )
    for q in col_peers:
        send(xbuf.at[c], xbuf.at[c], x_send.at[q], x_recv.at[c], (r, q))

    for cp in loads[1:]:
        cp.wait()
    factor = jnp.transpose(jnp.broadcast_to(gain_ref[...], (S, M)))
    shift = jnp.transpose(jnp.broadcast_to(shift_ref[...], (S, M)))
    mapping = map_ref[...]
    mapping_t = jnp.transpose(mapping.astype(F32)).astype(BF16)
    cotf[...] = cot_ref[...].astype(F32)
    cot = jnp.concatenate([cotf[pl.ds(j, BR, stride=BC), :] for j in range(BC)], axis=0).astype(BF16)
    w = w_ref[...]
    groups = K * K // 128
    G = dot(cot, w, 1, 1).astype(BF16).astype(F32)
    tiles = []
    for t in range(BC // 4):
        parts = []
        for j in range(4):
            row = (4 * t + j) * BR
            parts.append(jnp.stack([G[row:row + BR, 128 * g:128 * g + 128] for g in range(groups)], axis=0))
        b = swap_blocks(parts, K)
        tiles.append(jnp.stack(b, axis=1).reshape(K * BR, 128))
    g2 = jnp.concatenate(tiles, axis=1).astype(BF16)

    def standardized(x):
        mean = jnp.mean(x, axis=0, keepdims=True)
        cen = x - mean
        scale = lax.rsqrt(jnp.mean(cen * cen, axis=0, keepdims=True) + 1e-05)
        return cen * scale, scale

    own_unit, own_scale = standardized(xbuf[c].astype(F32))

    for q in col_peers:
        remote(xbuf.at[q], xbuf.at[q], x_send.at[q], x_recv.at[q], (r, q)).wait_recv()
    for k in range(BC):
        @pl.when(other(*owners[k]))
        def _():
            remote(
                xbuf.at[BR + k], xbuf.at[BR + k], x_send.at[0], x_recv.at[BR + k], owners[k]
            ).wait_recv()

    units, normeds = [], []
    for i in range(BR + BC):
        unit, _ = standardized(xbuf[i].astype(F32))
        units.append(unit)
        normeds.append((unit * factor + shift).astype(BF16))
    normed = jnp.concatenate(normeds, axis=1)
    proj = dot(mapping_t, normed, 1, 0)
    for i in range(BR):
        lf[pl.ds(i, K, stride=BR), :] = proj[:K, S * i:S * i + S].astype(BF16).astype(F32)
    left = lf[...].astype(BF16)
    right = jnp.concatenate(
        [proj[K:, S * (BR + j):S * (BR + j) + S] for j in range(BC)], axis=0
    ).astype(BF16)
    outer = (dot(left, right, 1, 1) * inv).astype(BF16).astype(F32)
    rows = []
    for t in range(BC // 4):
        o = outer[:, 128 * t:128 * t + 128].reshape(groups, 4, BR, 128)
        b = swap_blocks([o[:, q] for q in range(4)], K)
        for j in range(4):
            rows.append(jnp.concatenate([b[j][g] for g in range(groups)], axis=1))
    ot = jnp.concatenate(rows, axis=0).astype(BF16)

    wgrad = dot(ot, cot, 0, 0).astype(BF16)
    for p in range(R):
        s1[p] = wgrad[p * CH1:(p + 1) * CH1]
    for p in row_peers:
        send(s1.at[p], r1.at[r], s1_send.at[p], s1_recv.at[r], (p, c))

    glf[...] = dot(g2, right, 1, 0) * inv
    gr = (dot(g2, left, 0, 0) * inv).astype(BF16)
    gls = []
    for i in range(BR):
        gl = glf[pl.ds(i, K, stride=BR), :].astype(BF16)
        gls.append(gl)
        sl[i] = gl
    grs = []
    for j in range(BC):
        gg = gr[j * K:(j + 1) * K]
        grs.append(gg)
        sr[j] = gg
    rl[c] = sl[c]

    @pl.when(self_right)
    def _():
        rr[r] = sr[dest_slot]

    for q in col_peers:
        send(sl.at[q], rl.at[c], e_send.at[q], e_recv.at[c], (r, q))
    for k in range(BC):
        send(sr.at[k], rr.at[r], e_send.at[C + k], e_recv.at[C + r], owners[k], other(*owners[k]))

    glc = jnp.concatenate(gls, axis=1)
    grc = jnp.concatenate(grs, axis=1)
    cut = BR * S
    ebuf[...] = jnp.zeros_like(ebuf)
    ebuf[:, :K] = dot(normed[:, :cut], glc, 1, 1)
    ebuf[:, K:2 * K] = dot(normed[:, cut:], grc, 1, 1)
    gn = jnp.concatenate([dot(mapping[:, :K], glc, 1, 0), dot(mapping[:, K:], grc, 1, 0)], axis=1)
    bsum, gsum = jnp.zeros((M, S), F32), jnp.zeros((M, S), F32)
    for i in range(BR + BC):
        piece = gn[:, S * i:S * i + S]
        bsum = bsum + piece
        gsum = gsum + piece * units[i]
    ebuf[:, 2 * K:2 * K + 1] = jnp.sum(gsum, axis=1, keepdims=True)
    ebuf[:, 2 * K + 1:2 * K + 2] = jnp.sum(bsum, axis=1, keepdims=True)
    extra = ebuf[...].astype(BF16)
    for p in range(R):
        if p * EX < M:
            s1x[p] = extra[p * EX:(p + 1) * EX]
        else:
            s1x[p] = jnp.zeros((EX, 128), BF16)
    for p in row_peers:
        send(s1x.at[p], r1x.at[r], x1_send.at[p], x1_recv.at[r], (p, c))

    def total(buf, count):
        acc = buf[0].astype(F32)
        for p in range(1, count):
            acc = acc + buf[p].astype(F32)
        return acc

    r1[r] = s1[r]
    for p in row_peers:
        remote(s1.at[p], r1.at[p], s1_send.at[p], s1_recv.at[p], (p, c)).wait_recv()
    s2[...] = total(r1, R).astype(BF16)

    def chunk(q):
        return pl.ds(pl.multiple_of(lax.rem(q, NO) * CH2, 16), CH2)

    for q in col_peers:
        send(s2.at[chunk(q)], r2.at[c], s2_send.at[q], s2_recv.at[c], (r, q))
    r2[c] = s2[chunk(c)]

    r1x[r] = s1x[r]
    for p in row_peers:
        remote(s1x.at[p], r1x.at[p], x1_send.at[p], x1_recv.at[p], (p, c)).wait_recv()
    r2x[c] = total(r1x, R).astype(BF16)
    for q in col_peers:
        send(r2x.at[c], r2x.at[c], x2_send.at[q], x2_recv.at[c], (r, q))

    pairs = dot(ot, w, 1, 0) + bias_ref[...]
    for j in range(BC):
        pairf[pl.ds(j, BR, stride=BC), :] = pairs[j * BR:(j + 1) * BR]
    pair_ref[...] = pairf[...].astype(BF16)

    for q in col_peers:
        remote(s2.at[chunk(q)], r2.at[q], s2_send.at[q], s2_recv.at[q], (r, q)).wait_recv()

    mine = chunk(c)
    result = total(r2, C).astype(BF16)

    def forward(q):
        place = chunk(q)
        for p in row_peers:
            remote(
                gbuf.at[r, place], gbuf.at[r, place], g1_send.at[p * NO + q], g1_recv.at[r * NO + q], (p, c)
            ).start()

    def spread():
        gbuf[r, mine, :] = result
        for q in col_peers:
            remote(gbuf.at[r, mine], gbuf.at[r, mine], g2_send.at[q], g2_recv.at[c], (r, q)).start()
        forward(c)

    owning(c, spread)

    for q in col_peers:
        remote(r2x.at[q], r2x.at[q], x2_send.at[q], x2_recv.at[q], (r, q)).wait_recv()
    gx[r] = total(r2x, C).astype(BF16)
    for p in row_peers:
        send(gx.at[r], gx.at[r], x3_send.at[p], x3_recv.at[r], (p, c))

    for q in col_peers:
        remote(sl.at[q], rl.at[q], e_send.at[q], e_recv.at[q], (r, q)).wait_recv()
    for q in range(R):
        @pl.when(other(q, dest_col))
        def _():
            remote(sr.at[0], rr.at[q], e_send.at[C], e_recv.at[C + q], (q, dest_col)).wait_recv()
    act = jnp.concatenate([total(rl, C), total(rr, R)], axis=0).astype(BF16)
    scaled = dot(mapping, act, 1, 0) * factor
    align_ref[...] = own_scale * (
        scaled
        - jnp.mean(scaled, axis=0, keepdims=True)
        - own_unit * jnp.mean(scaled * own_unit, axis=0, keepdims=True)
    )

    for q in col_peers:
        def pass_on():
            place = chunk(q)
            remote(gbuf.at[r, place], gbuf.at[r, place], g2_send.at[q], g2_recv.at[q], (r, q)).wait_recv()
            forward(q)
        owning(q, pass_on)
    for p in row_peers:
        remote(gx.at[p], gx.at[p], x3_send.at[p], x3_recv.at[p], (p, c)).wait_recv()
        for q in range(NO):
            place = pl.ds(q * CH2, CH2)
            remote(
                gbuf.at[p, place], gbuf.at[p, place], g1_send.at[p * NO + q], g1_recv.at[p * NO + q], (p, c)
            ).wait_recv()
    gout_ref[...] = gbuf[...]
    gxout_ref[...] = gx[...]

    def spread_done():
        for q in col_peers:
            remote(gbuf.at[r, mine], gbuf.at[r, mine], g2_send.at[q], g2_recv.at[c], (r, q)).wait_send()

    owning(c, spread_done)
    for p in row_peers:
        for q in range(NO):
            place = pl.ds(q * CH2, CH2)
            remote(
                gbuf.at[r, place], gbuf.at[r, place], g1_send.at[p * NO + q], g1_recv.at[r * NO + q], (p, c)
            ).wait_send()
    for cp, cond in pending:
        if cond is None:
            cp.wait_send()
        else:
            pl.when(cond)(cp.wait_send)


def finish(cfg, pair_in, align_in, g_in, gx_in, pair_ref, align_ref, proj_ref, wg_ref, gg_ref, bg_ref):
    R, K, M, EX, CH1 = cfg
    pair_ref[...] = pair_in[...]
    align_ref[...] = align_in[...]
    for p in range(R):
        wg_ref[p * CH1:(p + 1) * CH1, :] = g_in[p].astype(F32)
    e = jnp.concatenate([gx_in[p].astype(F32) for p in range(M // EX)], axis=0)
    proj_ref[...] = e[:, :2 * K]
    flipped = jnp.transpose(e)
    gg_ref[...] = flipped[2 * K:2 * K + 1, :]
    bg_ref[...] = flipped[2 * K + 1:2 * K + 2, :]


def shards(x, gain, shift, mapping, w, bias, cot):
    R, C = lax.axis_size("row"), lax.axis_size("col")
    S, M = x.shape[0], x.shape[2]
    K = mapping.shape[1] // 2
    BR, BC, E = cot.shape
    rows = w.shape[0]
    CH1, EX = rows // R, max(16, M // R)
    CH2 = max(16, CH1 // C)
    NO = CH1 // CH2
    cfg = (R, C, BR, BC, S, M, K, CH1, EX, CH2, NO)
    vm = pl.BlockSpec(memory_space=pltpu.VMEM)
    hbm = pl.BlockSpec(memory_space=pltpu.HBM)
    sem = pltpu.SemaphoreType.DMA
    shape = jax.ShapeDtypeStruct
    params = pltpu.CompilerParams(
        collective_id=0, has_side_effects=True, vmem_limit_bytes=48 * 1024 * 1024
    )
    parts = pl.pallas_call(
        functools.partial(kernel, cfg),
        out_shape=[
            shape((BR * BC, E), BF16), shape((M, S), F32),
            shape((R, CH1, E), BF16), shape((R, EX, E), BF16),
        ],
        in_specs=[hbm] * 7,
        out_specs=[vm] * 4,
        scratch_shapes=[
            pltpu.VMEM((1, M), F32),
            pltpu.VMEM((1, M), F32),
            pltpu.VMEM(mapping.shape, BF16),
            pltpu.VMEM(w.shape, BF16),
            pltpu.VMEM((1, E), F32),
            pltpu.VMEM((BR * BC, E), BF16),
            pltpu.VMEM((BR + BC, M, S), BF16),
            pltpu.VMEM((K * BR, S), F32),
            pltpu.VMEM((BR * BC, E), F32),
            pltpu.VMEM((BR * BC, E), F32),
            pltpu.VMEM((K * BR, S), F32),
            pltpu.VMEM((BR, K, S), BF16),
            pltpu.VMEM((BC, K, S), BF16),
            pltpu.VMEM((C, K, S), BF16),
            pltpu.VMEM((R, K, S), BF16),
            pltpu.VMEM((R, CH1, E), BF16),
            pltpu.VMEM((R, CH1, E), BF16),
            pltpu.VMEM((CH1, E), BF16),
            pltpu.VMEM((C, CH2, E), BF16),
            pltpu.VMEM((R, CH1, E), BF16),
            pltpu.VMEM((M, E), F32),
            pltpu.VMEM((R, EX, E), BF16),
            pltpu.VMEM((R, EX, E), BF16),
            pltpu.VMEM((C, EX, E), BF16),
            pltpu.VMEM((R, EX, E), BF16),
            sem((7,)),
            sem((C + R,)), sem((BR + BC,)),
            sem((C + BC,)), sem((C + R,)),
            sem((R,)), sem((R,)),
            sem((C,)), sem((C,)),
            sem((C,)), sem((C,)),
            sem((R * NO,)), sem((R * NO,)),
            sem((R,)), sem((R,)),
            sem((C,)), sem((C,)),
            sem((R,)), sem((R,)),
        ],
        compiler_params=params,
        name="outer_mean",
    )(
        jnp.transpose(x, (1, 2, 0)).reshape(M, S), gain.reshape(1, M), shift.reshape(1, M), mapping, w,
        bias.reshape(1, E), cot.reshape(BR * BC, E),
    )
    pair, align, proj, wg, gg, bg = pl.pallas_call(
        functools.partial(finish, (R, K, M, EX, CH1)),
        out_shape=[
            shape((BR * BC, E), BF16), shape((M, S), F32), shape((M, 2 * K), F32),
            shape((rows, E), F32), shape((1, M), F32), shape((1, M), F32),
        ],
        in_specs=[vm] * 4,
        out_specs=[vm] * 6,
        compiler_params=pltpu.CompilerParams(vmem_limit_bytes=8 * 1024 * 1024),
        name="finish",
    )(*parts)
    return (
        pair.reshape(BR, BC, E), jnp.transpose(align.reshape(1, M, S), (2, 0, 1)), proj, wg,
        gg.reshape(M), bg.reshape(M),
    )


def solution(mesh):
    in_specs = (P(None, ("row", "col"), None), P(), P(), P(), P(), P(), P("row", "col", None))
    out_specs = (P("row", "col", None), P(None, ("row", "col"), None), P(), P(), P(), P())
    return jax.shard_map(shards, mesh=mesh, in_specs=in_specs, out_specs=out_specs, check_vma=False)
```

```python
import functools

import jax
import jax.numpy as jnp
from jax import lax
from jax.experimental import pallas as pl
from jax.experimental.pallas import tpu as pltpu
from jax.sharding import PartitionSpec as P

F32, BF16 = jnp.float32, jnp.bfloat16
MESH = pl.DeviceIdType.MESH


def swap_blocks(parts, width):
    axis = parts[0].ndim - 1
    lane = lax.broadcasted_iota(jnp.int32, parts[0].shape, axis)
    a0, a1, a2, a3 = parts
    total = 4 * width
    half = lane < 2 * width
    t0 = jnp.where(half, a0, pltpu.roll(a2, 2 * width, axis))
    t2 = jnp.where(half, pltpu.roll(a0, 2 * width, axis), a2)
    t1 = jnp.where(half, a1, pltpu.roll(a3, 2 * width, axis))
    t3 = jnp.where(half, pltpu.roll(a1, 2 * width, axis), a3)
    even = lane % (2 * width) < width
    u0 = jnp.where(even, t0, pltpu.roll(t1, width, axis))
    u1 = jnp.where(even, pltpu.roll(t0, total - width, axis), t1)
    u2 = jnp.where(even, t2, pltpu.roll(t3, width, axis))
    u3 = jnp.where(even, pltpu.roll(t2, total - width, axis), t3)
    return [u0, u1, u2, u3]


def dot(a, b, ca, cb):
    return lax.dot_general(a, b, (((ca,), (cb,)), ((), ())), preferred_element_type=F32)


def kernel(
    cfg, x_hbm, gain_hbm, shift_hbm, map_hbm, w_hbm, bias_hbm, cot_hbm,
    pair_ref, align_ref, gout_ref, gxout_ref,
    gain_ref, shift_ref, map_ref, w_ref, bias_ref, cot_ref,
    xown, lbuf, rbuf, lf, cotf, pairf, glf, sl, sr, rl, rr, s1, r1, s2, r2, gbuf, ebuf, s1x, r1x, r2x, gx, pr,
    load, x_send, x_recv, e_send, e_recv, s1_send, s1_recv, s2_send, s2_recv,
    g2_send, g2_recv, g1_send, g1_recv, x1_send, x1_recv, x2_send, x2_recv, x3_send, x3_recv,
):
    R, C, BR, BC, S, M, K, CH1, EX, CH2, NO = cfg
    r, c = lax.axis_index("row"), lax.axis_index("col")
    n = r * C + c
    dest_col, dest_slot = lax.div(n, BC), lax.rem(n, BC)
    self_right = dest_col == c
    inv = 1.0 / S
    row_peers = [lax.rem(r + off, R) for off in range(1, R)]
    col_peers = [lax.rem(c + off, C) for off in range(1, C)]

    loads = [
        pltpu.make_async_copy(src, dst, load.at[i])
        for i, (src, dst) in enumerate([
            (x_hbm, xown), (cot_hbm, cot_ref), (w_hbm, w_ref), (map_hbm, map_ref),
            (gain_hbm, gain_ref), (shift_hbm, shift_ref), (bias_hbm, bias_ref),
        ])
    ]
    for cp in loads:
        cp.start()

    def other(rr_, cc_):
        return jnp.logical_or(rr_ != r, cc_ != c)

    owners = []
    for k in range(BC):
        o = c * BC + k
        owners.append((lax.div(o, C), lax.rem(o, C)))

    def signal(dev):
        pl.semaphore_signal(barrier, inc=1, device_id=dev, device_id_type=MESH)

    def remote(src, dst, send, recv, dev):
        return pltpu.make_async_remote_copy(
            src_ref=src, dst_ref=dst, send_sem=send, recv_sem=recv, device_id=dev, device_id_type=MESH
        )

    def owning(q, f):
        if NO == C:
            f()
        else:
            pl.when(q < NO)(f)

    barrier = pltpu.get_barrier_semaphore()
    for q in col_peers:
        signal((r, q))
    for p in row_peers:
        signal((p, c))
    for q in range(R):
        @pl.when(other(q, dest_col))
        def _():
            signal((q, dest_col))
    for k in range(BC):
        @pl.when(other(*owners[k]))
        def _():
            signal(owners[k])

    def standardized(x):
        mean = jnp.mean(x, axis=0, keepdims=True)
        cen = x - mean
        scale = lax.rsqrt(jnp.mean(cen * cen, axis=0, keepdims=True) + 1e-05)
        return cen * scale, scale

    early = (0, 3, 4, 5)
    for i in early:
        loads[i].wait()
    factor = jnp.transpose(jnp.broadcast_to(gain_ref[...], (S, M)))
    shift = jnp.transpose(jnp.broadcast_to(shift_ref[...], (S, M)))
    mapping = map_ref[...]
    mapping_t = jnp.transpose(mapping.astype(F32)).astype(BF16)
    own_unit, own_scale = standardized(xown[...].astype(F32))
    normed = (own_unit * factor + shift).astype(BF16)
    proj = dot(mapping_t, normed, 1, 0).astype(BF16)
    lbuf[c] = proj[:K]
    pr[...] = proj[K:]

    @pl.when(self_right)
    def _():
        rbuf[dest_slot] = proj[K:]

    pl.semaphore_wait(barrier, C - 1 + R - 1 + R + BC - jnp.where(self_right, 2, 0))

    pending = []

    def send(src, dst, ssem, rsem, dev, cond=None):
        cp = remote(src, dst, ssem, rsem, dev)
        if cond is None:
            cp.start()
        else:
            pl.when(cond)(cp.start)
        pending.append((cp, cond))

    for q in range(R):
        send(
            pr, rbuf.at[dest_slot], x_send.at[C + q], x_recv.at[BR + dest_slot],
            (q, dest_col), other(q, dest_col),
        )
    for q in col_peers:
        send(lbuf.at[c], lbuf.at[c], x_send.at[q], x_recv.at[c], (r, q))

    for i in range(len(loads)):
        if i not in early:
            loads[i].wait()
    cotf[...] = cot_ref[...].astype(F32)
    cot = jnp.concatenate([cotf[pl.ds(j, BR, stride=BC), :] for j in range(BC)], axis=0).astype(BF16)
    w = w_ref[...]
    groups = K * K // 128
    G = dot(cot, w, 1, 1).astype(BF16).astype(F32)
    tiles = []
    for t in range(BC // 4):
        parts = []
        for j in range(4):
            row = (4 * t + j) * BR
            parts.append(jnp.stack([G[row:row + BR, 128 * g:128 * g + 128] for g in range(groups)], axis=0))
        b = swap_blocks(parts, K)
        tiles.append(jnp.stack(b, axis=1).reshape(K * BR, 128))
    g2 = jnp.concatenate(tiles, axis=1).astype(BF16)

    for q in col_peers:
        remote(lbuf.at[q], lbuf.at[q], x_send.at[q], x_recv.at[q], (r, q)).wait_recv()
    for k in range(BC):
        @pl.when(other(*owners[k]))
        def _():
            remote(
                rbuf.at[k], rbuf.at[k], x_send.at[0], x_recv.at[BR + k], owners[k]
            ).wait_recv()

    for i in range(BR):
        lf[pl.ds(i, K, stride=BR), :] = lbuf[i].astype(F32)
    left = lf[...].astype(BF16)
    right = jnp.concatenate([rbuf[j] for j in range(BC)], axis=0)
    outer = (dot(left, right, 1, 1) * inv).astype(BF16).astype(F32)
    rows = []
    for t in range(BC // 4):
        o = outer[:, 128 * t:128 * t + 128].reshape(groups, 4, BR, 128)
        b = swap_blocks([o[:, q] for q in range(4)], K)
        for j in range(4):
            rows.append(jnp.concatenate([b[j][g] for g in range(groups)], axis=1))
    ot = jnp.concatenate(rows, axis=0).astype(BF16)

    wgrad = dot(ot, cot, 0, 0).astype(BF16)
    for p in range(R):
        s1[p] = wgrad[p * CH1:(p + 1) * CH1]
    for p in row_peers:
        send(s1.at[p], r1.at[r], s1_send.at[p], s1_recv.at[r], (p, c))

    glf[...] = dot(g2, right, 1, 0) * inv
    gr = (dot(g2, left, 0, 0) * inv).astype(BF16)
    for i in range(BR):
        gl = glf[pl.ds(i, K, stride=BR), :].astype(BF16)
        sl[i] = gl
    for j in range(BC):
        gg = gr[j * K:(j + 1) * K]
        sr[j] = gg
    rl[c] = sl[c]

    @pl.when(self_right)
    def _():
        rr[r] = sr[dest_slot]

    for q in col_peers:
        send(sl.at[q], rl.at[c], e_send.at[q], e_recv.at[c], (r, q))
    for k in range(BC):
        send(sr.at[k], rr.at[r], e_send.at[C + k], e_recv.at[C + r], owners[k], other(*owners[k]))

    def total(buf, count):
        acc = buf[0].astype(F32)
        for p in range(1, count):
            acc = acc + buf[p].astype(F32)
        return acc

    r1[r] = s1[r]
    for p in row_peers:
        remote(s1.at[p], r1.at[p], s1_send.at[p], s1_recv.at[p], (p, c)).wait_recv()
    s2[...] = total(r1, R).astype(BF16)

    def chunk(q):
        return pl.ds(pl.multiple_of(lax.rem(q, NO) * CH2, 16), CH2)

    for q in col_peers:
        send(s2.at[chunk(q)], r2.at[c], s2_send.at[q], s2_recv.at[c], (r, q))
    r2[c] = s2[chunk(c)]

    for q in col_peers:
        remote(sl.at[q], rl.at[q], e_send.at[q], e_recv.at[q], (r, q)).wait_recv()
    for q in range(R):
        @pl.when(other(q, dest_col))
        def _():
            remote(sr.at[0], rr.at[q], e_send.at[C], e_recv.at[C + q], (q, dest_col)).wait_recv()
    act = jnp.concatenate([total(rl, C), total(rr, R)], axis=0).astype(BF16)
    grad_normed = dot(mapping, act, 1, 0)
    ebuf[...] = jnp.zeros_like(ebuf)
    ebuf[:, :2 * K] = dot(normed, act, 1, 1)
    ebuf[:, 2 * K:2 * K + 1] = jnp.sum(grad_normed * own_unit, axis=1, keepdims=True)
    ebuf[:, 2 * K + 1:2 * K + 2] = jnp.sum(grad_normed, axis=1, keepdims=True)
    extra = ebuf[...].astype(BF16)
    for p in range(R):
        if p * EX < M:
            s1x[p] = extra[p * EX:(p + 1) * EX]
        else:
            s1x[p] = jnp.zeros((EX, 128), BF16)
    for p in row_peers:
        send(s1x.at[p], r1x.at[r], x1_send.at[p], x1_recv.at[r], (p, c))
    scaled = grad_normed * factor
    align_ref[...] = own_scale * (
        scaled
        - jnp.mean(scaled, axis=0, keepdims=True)
        - own_unit * jnp.mean(scaled * own_unit, axis=0, keepdims=True)
    )

    pairs = dot(ot, w, 1, 0) + bias_ref[...]
    for j in range(BC):
        pairf[pl.ds(j, BR, stride=BC), :] = pairs[j * BR:(j + 1) * BR]
    pair_ref[...] = pairf[...].astype(BF16)

    r1x[r] = s1x[r]
    for p in row_peers:
        remote(s1x.at[p], r1x.at[p], x1_send.at[p], x1_recv.at[p], (p, c)).wait_recv()
    r2x[c] = total(r1x, R).astype(BF16)
    for q in col_peers:
        send(r2x.at[c], r2x.at[c], x2_send.at[q], x2_recv.at[c], (r, q))

    for q in col_peers:
        remote(s2.at[chunk(q)], r2.at[q], s2_send.at[q], s2_recv.at[q], (r, q)).wait_recv()

    mine = chunk(c)
    result = total(r2, C).astype(BF16)

    def forward(q):
        place = chunk(q)
        for p in row_peers:
            remote(
                gbuf.at[r, place], gbuf.at[r, place], g1_send.at[p * NO + q], g1_recv.at[r * NO + q], (p, c)
            ).start()

    def spread():
        gbuf[r, mine, :] = result
        for q in col_peers:
            remote(gbuf.at[r, mine], gbuf.at[r, mine], g2_send.at[q], g2_recv.at[c], (r, q)).start()
        forward(c)

    owning(c, spread)

    for q in col_peers:
        remote(r2x.at[q], r2x.at[q], x2_send.at[q], x2_recv.at[q], (r, q)).wait_recv()
    gx[r] = total(r2x, C).astype(BF16)
    for p in row_peers:
        send(gx.at[r], gx.at[r], x3_send.at[p], x3_recv.at[r], (p, c))

    for q in col_peers:
        def pass_on():
            place = chunk(q)
            remote(gbuf.at[r, place], gbuf.at[r, place], g2_send.at[q], g2_recv.at[q], (r, q)).wait_recv()
            forward(q)
        owning(q, pass_on)
    for p in row_peers:
        remote(gx.at[p], gx.at[p], x3_send.at[p], x3_recv.at[p], (p, c)).wait_recv()
        for q in range(NO):
            place = pl.ds(q * CH2, CH2)
            remote(
                gbuf.at[p, place], gbuf.at[p, place], g1_send.at[p * NO + q], g1_recv.at[p * NO + q], (p, c)
            ).wait_recv()
    gout_ref[...] = gbuf[...]
    gxout_ref[...] = gx[...]

    def spread_done():
        for q in col_peers:
            remote(gbuf.at[r, mine], gbuf.at[r, mine], g2_send.at[q], g2_recv.at[c], (r, q)).wait_send()

    owning(c, spread_done)
    for p in row_peers:
        for q in range(NO):
            place = pl.ds(q * CH2, CH2)
            remote(
                gbuf.at[r, place], gbuf.at[r, place], g1_send.at[p * NO + q], g1_recv.at[r * NO + q], (p, c)
            ).wait_send()
    for cp, cond in pending:
        if cond is None:
            cp.wait_send()
        else:
            pl.when(cond)(cp.wait_send)


def finish(cfg, pair_in, align_in, g_in, gx_in, pair_ref, align_ref, proj_ref, wg_ref, gg_ref, bg_ref):
    R, K, M, EX, CH1 = cfg
    pair_ref[...] = pair_in[...]
    align_ref[...] = align_in[...]
    for p in range(R):
        wg_ref[p * CH1:(p + 1) * CH1, :] = g_in[p].astype(F32)
    e = jnp.concatenate([gx_in[p].astype(F32) for p in range(M // EX)], axis=0)
    proj_ref[...] = e[:, :2 * K]
    flipped = jnp.transpose(e)
    gg_ref[...] = flipped[2 * K:2 * K + 1, :]
    bg_ref[...] = flipped[2 * K + 1:2 * K + 2, :]


def shards(x, gain, shift, mapping, w, bias, cot):
    R, C = lax.axis_size("row"), lax.axis_size("col")
    S, M = x.shape[0], x.shape[2]
    K = mapping.shape[1] // 2
    BR, BC, E = cot.shape
    rows = w.shape[0]
    CH1, EX = rows // R, max(16, M // R)
    CH2 = max(16, CH1 // C)
    NO = CH1 // CH2
    cfg = (R, C, BR, BC, S, M, K, CH1, EX, CH2, NO)
    vm = pl.BlockSpec(memory_space=pltpu.VMEM)
    hbm = pl.BlockSpec(memory_space=pltpu.HBM)
    sem = pltpu.SemaphoreType.DMA
    shape = jax.ShapeDtypeStruct
    params = pltpu.CompilerParams(
        collective_id=0, has_side_effects=True, vmem_limit_bytes=58 * 1024 * 1024
    )
    parts = pl.pallas_call(
        functools.partial(kernel, cfg),
        out_shape=[
            shape((BR * BC, E), BF16), shape((M, S), F32),
            shape((R, CH1, E), BF16), shape((R, EX, E), BF16),
        ],
        in_specs=[hbm] * 7,
        out_specs=[vm] * 4,
        scratch_shapes=[
            pltpu.VMEM((1, M), F32),
            pltpu.VMEM((1, M), F32),
            pltpu.VMEM(mapping.shape, BF16),
            pltpu.VMEM(w.shape, BF16),
            pltpu.VMEM((1, E), F32),
            pltpu.VMEM((BR * BC, E), BF16),
            pltpu.VMEM((M, S), BF16),
            pltpu.VMEM((BR, K, S), BF16),
            pltpu.VMEM((BC, K, S), BF16),
            pltpu.VMEM((K * BR, S), F32),
            pltpu.VMEM((BR * BC, E), F32),
            pltpu.VMEM((BR * BC, E), F32),
            pltpu.VMEM((K * BR, S), F32),
            pltpu.VMEM((BR, K, S), BF16),
            pltpu.VMEM((BC, K, S), BF16),
            pltpu.VMEM((C, K, S), BF16),
            pltpu.VMEM((R, K, S), BF16),
            pltpu.VMEM((R, CH1, E), BF16),
            pltpu.VMEM((R, CH1, E), BF16),
            pltpu.VMEM((CH1, E), BF16),
            pltpu.VMEM((C, CH2, E), BF16),
            pltpu.VMEM((R, CH1, E), BF16),
            pltpu.VMEM((M, E), F32),
            pltpu.VMEM((R, EX, E), BF16),
            pltpu.VMEM((R, EX, E), BF16),
            pltpu.VMEM((C, EX, E), BF16),
            pltpu.VMEM((R, EX, E), BF16),
            pltpu.VMEM((K, S), BF16),
            sem((7,)),
            sem((C + R,)), sem((BR + BC,)),
            sem((C + BC,)), sem((C + R,)),
            sem((R,)), sem((R,)),
            sem((C,)), sem((C,)),
            sem((C,)), sem((C,)),
            sem((R * NO,)), sem((R * NO,)),
            sem((R,)), sem((R,)),
            sem((C,)), sem((C,)),
            sem((R,)), sem((R,)),
        ],
        compiler_params=params,
        name="outer_mean",
    )(
        jnp.transpose(x, (1, 2, 0)).reshape(M, S), gain.reshape(1, M), shift.reshape(1, M), mapping, w,
        bias.reshape(1, E), cot.reshape(BR * BC, E),
    )
    pair, align, proj, wg, gg, bg = pl.pallas_call(
        functools.partial(finish, (R, K, M, EX, CH1)),
        out_shape=[
            shape((BR * BC, E), BF16), shape((M, S), F32), shape((M, 2 * K), F32),
            shape((rows, E), F32), shape((1, M), F32), shape((1, M), F32),
        ],
        in_specs=[vm] * 4,
        out_specs=[vm] * 6,
        compiler_params=pltpu.CompilerParams(vmem_limit_bytes=58 * 1024 * 1024),
        name="finish",
    )(*parts)
    return (
        pair.reshape(BR, BC, E), jnp.transpose(align.reshape(1, M, S), (2, 0, 1)), proj, wg,
        gg.reshape(M), bg.reshape(M),
    )


def solution(mesh):
    in_specs = (P(None, ("row", "col"), None), P(), P(), P(), P(), P(), P("row", "col", None))
    out_specs = (P("row", "col", None), P(None, ("row", "col"), None), P(), P(), P(), P())
    return jax.shard_map(shards, mesh=mesh, in_specs=in_specs, out_specs=out_specs, check_vma=False)
```

```python
import functools

import jax
import jax.numpy as jnp
from jax import lax
from jax.experimental import pallas as pl
from jax.experimental.pallas import tpu as pltpu
from jax.sharding import PartitionSpec as P

F32, BF16 = jnp.float32, jnp.bfloat16
MESH = pl.DeviceIdType.MESH


def swap_blocks(parts, width):
    axis = parts[0].ndim - 1
    lane = lax.broadcasted_iota(jnp.int32, parts[0].shape, axis)
    a0, a1, a2, a3 = parts
    total = 4 * width
    half = lane < 2 * width
    t0 = jnp.where(half, a0, pltpu.roll(a2, 2 * width, axis))
    t2 = jnp.where(half, pltpu.roll(a0, 2 * width, axis), a2)
    t1 = jnp.where(half, a1, pltpu.roll(a3, 2 * width, axis))
    t3 = jnp.where(half, pltpu.roll(a1, 2 * width, axis), a3)
    even = lane % (2 * width) < width
    u0 = jnp.where(even, t0, pltpu.roll(t1, width, axis))
    u1 = jnp.where(even, pltpu.roll(t0, total - width, axis), t1)
    u2 = jnp.where(even, t2, pltpu.roll(t3, width, axis))
    u3 = jnp.where(even, pltpu.roll(t2, total - width, axis), t3)
    return [u0, u1, u2, u3]


def dot(a, b, ca, cb):
    return lax.dot_general(a, b, (((ca,), (cb,)), ((), ())), preferred_element_type=F32)


def kernel(
    cfg, x_hbm, gain_hbm, shift_hbm, map_hbm, w_hbm, bias_hbm, cot_hbm,
    pair_ref, align_ref, gout_ref, gxout_ref,
    gain_ref, shift_ref, map_ref, w_ref, bias_ref, cot_ref,
    xown, lbuf, rbuf, lf, cotf, pairf, glf, sl, sr, rl, rr, s1, r1, s2, r2, gbuf, ebuf, s1x, r1x, r2x, gx, pr, alignf, pairb, store,
    load, x_send, x_recv, e_send, e_recv, s1_send, s1_recv, s2_send, s2_recv,
    g2_send, g2_recv, g1_send, g1_recv, x1_send, x1_recv, x2_send, x2_recv, x3_send, x3_recv,
):
    R, C, BR, BC, S, M, K, CH1, EX, CH2, NO = cfg
    r, c = lax.axis_index("row"), lax.axis_index("col")
    n = r * C + c
    dest_col, dest_slot = lax.div(n, BC), lax.rem(n, BC)
    self_right = dest_col == c
    inv = 1.0 / S
    row_peers = [lax.rem(r + off, R) for off in range(1, R)]
    col_peers = [lax.rem(c + off, C) for off in range(1, C)]

    loads = [
        pltpu.make_async_copy(src, dst, load.at[i])
        for i, (src, dst) in enumerate([
            (x_hbm, xown), (cot_hbm, cot_ref), (w_hbm, w_ref), (map_hbm, map_ref),
            (gain_hbm, gain_ref), (shift_hbm, shift_ref), (bias_hbm, bias_ref),
        ])
    ]
    for cp in loads:
        cp.start()

    def other(rr_, cc_):
        return jnp.logical_or(rr_ != r, cc_ != c)

    owners = []
    for k in range(BC):
        o = c * BC + k
        owners.append((lax.div(o, C), lax.rem(o, C)))

    def signal(dev):
        pl.semaphore_signal(barrier, inc=1, device_id=dev, device_id_type=MESH)

    def remote(src, dst, send, recv, dev):
        return pltpu.make_async_remote_copy(
            src_ref=src, dst_ref=dst, send_sem=send, recv_sem=recv, device_id=dev, device_id_type=MESH
        )

    def owning(q, f):
        if NO == C:
            f()
        else:
            pl.when(q < NO)(f)

    barrier = pltpu.get_barrier_semaphore()
    for q in col_peers:
        signal((r, q))
    for p in row_peers:
        signal((p, c))
    for q in range(R):
        @pl.when(other(q, dest_col))
        def _():
            signal((q, dest_col))
    for k in range(BC):
        @pl.when(other(*owners[k]))
        def _():
            signal(owners[k])

    def standardized(x):
        mean = jnp.mean(x, axis=0, keepdims=True)
        cen = x - mean
        scale = lax.rsqrt(jnp.mean(cen * cen, axis=0, keepdims=True) + 1e-05)
        return cen * scale, scale

    early = (0, 3, 4, 5)
    for i in early:
        loads[i].wait()
    factor = jnp.transpose(jnp.broadcast_to(gain_ref[...], (S, M)))
    shift = jnp.transpose(jnp.broadcast_to(shift_ref[...], (S, M)))
    mapping = map_ref[...]
    mapping_t = jnp.transpose(mapping.astype(F32)).astype(BF16)
    own_unit, own_scale = standardized(xown[...].astype(F32))
    normed = (own_unit * factor + shift).astype(BF16)
    proj = dot(mapping_t, normed, 1, 0).astype(BF16)
    lbuf[c] = proj[:K]
    pr[...] = proj[K:]

    @pl.when(self_right)
    def _():
        rbuf[dest_slot] = proj[K:]

    pl.semaphore_wait(barrier, C - 1 + R - 1 + R + BC - jnp.where(self_right, 2, 0))

    pending = []

    def send(src, dst, ssem, rsem, dev, cond=None):
        cp = remote(src, dst, ssem, rsem, dev)
        if cond is None:
            cp.start()
        else:
            pl.when(cond)(cp.start)
        pending.append((cp, cond))

    for q in range(R):
        send(
            pr, rbuf.at[dest_slot], x_send.at[C + q], x_recv.at[BR + dest_slot],
            (q, dest_col), other(q, dest_col),
        )
    for q in col_peers:
        send(lbuf.at[c], lbuf.at[c], x_send.at[q], x_recv.at[c], (r, q))

    for i in range(len(loads)):
        if i not in early:
            loads[i].wait()
    cotf[...] = cot_ref[...].astype(F32)
    cot = jnp.concatenate([cotf[pl.ds(j, BR, stride=BC), :] for j in range(BC)], axis=0).astype(BF16)
    w = w_ref[...]
    groups = K * K // 128
    G = dot(cot, w, 1, 1).astype(BF16).astype(F32)
    tiles = []
    for t in range(BC // 4):
        parts = []
        for j in range(4):
            row = (4 * t + j) * BR
            parts.append(jnp.stack([G[row:row + BR, 128 * g:128 * g + 128] for g in range(groups)], axis=0))
        b = swap_blocks(parts, K)
        tiles.append(jnp.stack(b, axis=1).reshape(K * BR, 128))
    g2 = jnp.concatenate(tiles, axis=1).astype(BF16)

    for q in col_peers:
        remote(lbuf.at[q], lbuf.at[q], x_send.at[q], x_recv.at[q], (r, q)).wait_recv()
    for k in range(BC):
        @pl.when(other(*owners[k]))
        def _():
            remote(
                rbuf.at[k], rbuf.at[k], x_send.at[0], x_recv.at[BR + k], owners[k]
            ).wait_recv()

    for i in range(BR):
        lf[pl.ds(i, K, stride=BR), :] = lbuf[i].astype(F32)
    left = lf[...].astype(BF16)
    right = jnp.concatenate([rbuf[j] for j in range(BC)], axis=0)
    outer = (dot(left, right, 1, 1) * inv).astype(BF16).astype(F32)
    rows = []
    for t in range(BC // 4):
        o = outer[:, 128 * t:128 * t + 128].reshape(groups, 4, BR, 128)
        b = swap_blocks([o[:, q] for q in range(4)], K)
        for j in range(4):
            rows.append(jnp.concatenate([b[j][g] for g in range(groups)], axis=1))
    ot = jnp.concatenate(rows, axis=0).astype(BF16)

    wgrad = dot(ot, cot, 0, 0).astype(BF16)
    for p in range(R):
        s1[p] = wgrad[p * CH1:(p + 1) * CH1]
    for p in row_peers:
        send(s1.at[p], r1.at[r], s1_send.at[p], s1_recv.at[r], (p, c))

    glf[...] = dot(g2, right, 1, 0) * inv
    gr = (dot(g2, left, 0, 0) * inv).astype(BF16)
    for i in range(BR):
        gl = glf[pl.ds(i, K, stride=BR), :].astype(BF16)
        sl[i] = gl
    for j in range(BC):
        gg = gr[j * K:(j + 1) * K]
        sr[j] = gg
    rl[c] = sl[c]

    @pl.when(self_right)
    def _():
        rr[r] = sr[dest_slot]

    for q in col_peers:
        send(sl.at[q], rl.at[c], e_send.at[q], e_recv.at[c], (r, q))
    for k in range(BC):
        send(sr.at[k], rr.at[r], e_send.at[C + k], e_recv.at[C + r], owners[k], other(*owners[k]))

    def total(buf, count):
        acc = buf[0].astype(F32)
        for p in range(1, count):
            acc = acc + buf[p].astype(F32)
        return acc

    r1[r] = s1[r]
    for p in row_peers:
        remote(s1.at[p], r1.at[p], s1_send.at[p], s1_recv.at[p], (p, c)).wait_recv()
    s2[...] = total(r1, R).astype(BF16)

    def chunk(q):
        return pl.ds(pl.multiple_of(lax.rem(q, NO) * CH2, 16), CH2)

    for q in col_peers:
        send(s2.at[chunk(q)], r2.at[c], s2_send.at[q], s2_recv.at[c], (r, q))
    r2[c] = s2[chunk(c)]

    for q in col_peers:
        remote(sl.at[q], rl.at[q], e_send.at[q], e_recv.at[q], (r, q)).wait_recv()
    for q in range(R):
        @pl.when(other(q, dest_col))
        def _():
            remote(sr.at[0], rr.at[q], e_send.at[C], e_recv.at[C + q], (q, dest_col)).wait_recv()
    act = jnp.concatenate([total(rl, C), total(rr, R)], axis=0).astype(BF16)
    grad_normed = dot(mapping, act, 1, 0)
    ebuf[...] = jnp.zeros_like(ebuf)
    ebuf[:, :2 * K] = dot(normed, act, 1, 1)
    ebuf[:, 2 * K:2 * K + 1] = jnp.sum(grad_normed * own_unit, axis=1, keepdims=True)
    ebuf[:, 2 * K + 1:2 * K + 2] = jnp.sum(grad_normed, axis=1, keepdims=True)
    extra = ebuf[...].astype(BF16)
    for p in range(R):
        if p * EX < M:
            s1x[p] = extra[p * EX:(p + 1) * EX]
        else:
            s1x[p] = jnp.zeros((EX, 128), BF16)
    for p in row_peers:
        send(s1x.at[p], r1x.at[r], x1_send.at[p], x1_recv.at[r], (p, c))
    scaled = grad_normed * factor
    alignf[...] = own_scale * (
        scaled
        - jnp.mean(scaled, axis=0, keepdims=True)
        - own_unit * jnp.mean(scaled * own_unit, axis=0, keepdims=True)
    )

    stores = [pltpu.make_async_copy(alignf, align_ref, store.at[0])]
    stores[0].start()
    pairs = dot(ot, w, 1, 0) + bias_ref[...]
    for j in range(BC):
        pairf[pl.ds(j, BR, stride=BC), :] = pairs[j * BR:(j + 1) * BR]
    pairb[...] = pairf[...].astype(BF16)
    stores.append(pltpu.make_async_copy(pairb, pair_ref, store.at[1]))
    stores[1].start()

    r1x[r] = s1x[r]
    for p in row_peers:
        remote(s1x.at[p], r1x.at[p], x1_send.at[p], x1_recv.at[p], (p, c)).wait_recv()
    r2x[c] = total(r1x, R).astype(BF16)
    for q in col_peers:
        send(r2x.at[c], r2x.at[c], x2_send.at[q], x2_recv.at[c], (r, q))

    for q in col_peers:
        remote(s2.at[chunk(q)], r2.at[q], s2_send.at[q], s2_recv.at[q], (r, q)).wait_recv()

    mine = chunk(c)
    result = total(r2, C).astype(BF16)

    half = NO // 2
    near = lax.div(lax.rem(c, NO), half)

    def group(h):
        return pl.ds(pl.multiple_of(h * half * CH2, 16), half * CH2)

    def forward(h, p):
        return remote(
            gbuf.at[r, group(h)], gout_ref.at[r, group(h)], g1_send.at[p * 2 + h], g1_recv.at[r * 2 + h], (p, c)
        )

    def spread():
        gbuf[r, mine, :] = result
        for q in col_peers:
            remote(gbuf.at[r, mine], gbuf.at[r, mine], g2_send.at[q], g2_recv.at[c], (r, q)).start()

    owning(c, spread)

    for q in col_peers:
        remote(r2x.at[q], r2x.at[q], x2_send.at[q], x2_recv.at[q], (r, q)).wait_recv()
    gx[r] = total(r2x, C).astype(BF16)
    for p in row_peers:
        send(gx.at[r], gxout_ref.at[r], x3_send.at[p], x3_recv.at[r], (p, c))
    stores.append(pltpu.make_async_copy(gx.at[r], gxout_ref.at[r], store.at[3]))
    stores[-1].start()

    for h in (near, 1 - near):
        for t in range(half):
            q = h * half + t

            @pl.when(q != c)
            def _():
                place = chunk(q)
                remote(gbuf.at[r, place], gbuf.at[r, place], g2_send.at[q], g2_recv.at[q], (r, q)).wait_recv()
        for p in row_peers:
            forward(h, p).start()
    stores.append(pltpu.make_async_copy(gbuf.at[r], gout_ref.at[r], store.at[2]))
    stores[-1].start()
    for p in row_peers:
        remote(gx.at[p], gxout_ref.at[p], x3_send.at[p], x3_recv.at[p], (p, c)).wait_recv()
        for h in range(2):
            remote(
                gbuf.at[p, group(h)], gout_ref.at[p, group(h)], g1_send.at[p * 2 + h], g1_recv.at[p * 2 + h], (p, c)
            ).wait_recv()
    for cp in stores:
        cp.wait()

    def spread_done():
        for q in col_peers:
            remote(gbuf.at[r, mine], gbuf.at[r, mine], g2_send.at[q], g2_recv.at[c], (r, q)).wait_send()

    owning(c, spread_done)
    for p in row_peers:
        for h in range(2):
            forward(h, p).wait_send()
    for cp, cond in pending:
        if cond is None:
            cp.wait_send()
        else:
            pl.when(cond)(cp.wait_send)


def finish(cfg, pair_in, align_in, g_in, gx_in, pair_ref, align_ref, proj_ref, wg_ref, gg_ref, bg_ref):
    R, K, M, EX, CH1 = cfg
    pair_ref[...] = pair_in[...]
    align_ref[...] = align_in[...]
    for p in range(R):
        wg_ref[p * CH1:(p + 1) * CH1, :] = g_in[p].astype(F32)
    e = jnp.concatenate([gx_in[p].astype(F32) for p in range(M // EX)], axis=0)
    proj_ref[...] = e[:, :2 * K]
    flipped = jnp.transpose(e)
    gg_ref[...] = flipped[2 * K:2 * K + 1, :]
    bg_ref[...] = flipped[2 * K + 1:2 * K + 2, :]


def shards(x, gain, shift, mapping, w, bias, cot):
    R, C = lax.axis_size("row"), lax.axis_size("col")
    S, M = x.shape[0], x.shape[2]
    K = mapping.shape[1] // 2
    BR, BC, E = cot.shape
    rows = w.shape[0]
    CH1, EX = rows // R, max(16, M // R)
    CH2 = max(16, CH1 // C)
    NO = CH1 // CH2
    cfg = (R, C, BR, BC, S, M, K, CH1, EX, CH2, NO)
    vm = pl.BlockSpec(memory_space=pltpu.VMEM)
    hbm = pl.BlockSpec(memory_space=pltpu.HBM)
    sem = pltpu.SemaphoreType.DMA
    shape = jax.ShapeDtypeStruct
    params = pltpu.CompilerParams(
        collective_id=0, has_side_effects=True, vmem_limit_bytes=58 * 1024 * 1024
    )
    parts = pl.pallas_call(
        functools.partial(kernel, cfg),
        out_shape=[
            shape((BR * BC, E), BF16), shape((M, S), F32),
            shape((R, CH1, E), BF16), shape((R, EX, E), BF16),
        ],
        in_specs=[hbm] * 7,
        out_specs=[hbm] * 4,
        scratch_shapes=[
            pltpu.VMEM((1, M), F32),
            pltpu.VMEM((1, M), F32),
            pltpu.VMEM(mapping.shape, BF16),
            pltpu.VMEM(w.shape, BF16),
            pltpu.VMEM((1, E), F32),
            pltpu.VMEM((BR * BC, E), BF16),
            pltpu.VMEM((M, S), BF16),
            pltpu.VMEM((BR, K, S), BF16),
            pltpu.VMEM((BC, K, S), BF16),
            pltpu.VMEM((K * BR, S), F32),
            pltpu.VMEM((BR * BC, E), F32),
            pltpu.VMEM((BR * BC, E), F32),
            pltpu.VMEM((K * BR, S), F32),
            pltpu.VMEM((BR, K, S), BF16),
            pltpu.VMEM((BC, K, S), BF16),
            pltpu.VMEM((C, K, S), BF16),
            pltpu.VMEM((R, K, S), BF16),
            pltpu.VMEM((R, CH1, E), BF16),
            pltpu.VMEM((R, CH1, E), BF16),
            pltpu.VMEM((CH1, E), BF16),
            pltpu.VMEM((C, CH2, E), BF16),
            pltpu.VMEM((R, CH1, E), BF16),
            pltpu.VMEM((M, E), F32),
            pltpu.VMEM((R, EX, E), BF16),
            pltpu.VMEM((R, EX, E), BF16),
            pltpu.VMEM((C, EX, E), BF16),
            pltpu.VMEM((R, EX, E), BF16),
            pltpu.VMEM((K, S), BF16),
            pltpu.VMEM((M, S), F32),
            pltpu.VMEM((BR * BC, E), BF16),
            sem((4,)),
            sem((7,)),
            sem((C + R,)), sem((BR + BC,)),
            sem((C + BC,)), sem((C + R,)),
            sem((R,)), sem((R,)),
            sem((C,)), sem((C,)),
            sem((C,)), sem((C,)),
            sem((R * 2,)), sem((R * 2,)),
            sem((R,)), sem((R,)),
            sem((C,)), sem((C,)),
            sem((R,)), sem((R,)),
        ],
        compiler_params=params,
        name="outer_mean",
    )(
        jnp.transpose(x, (1, 2, 0)).reshape(M, S), gain.reshape(1, M), shift.reshape(1, M), mapping, w,
        bias.reshape(1, E), cot.reshape(BR * BC, E),
    )
    pair, align, proj, wg, gg, bg = pl.pallas_call(
        functools.partial(finish, (R, K, M, EX, CH1)),
        out_shape=[
            shape((BR * BC, E), BF16), shape((M, S), F32), shape((M, 2 * K), F32),
            shape((rows, E), F32), shape((1, M), F32), shape((1, M), F32),
        ],
        in_specs=[vm] * 4,
        out_specs=[vm] * 6,
        compiler_params=pltpu.CompilerParams(vmem_limit_bytes=58 * 1024 * 1024),
        name="finish",
    )(*parts)
    return (
        pair.reshape(BR, BC, E), jnp.transpose(align.reshape(1, M, S), (2, 0, 1)), proj, wg,
        gg.reshape(M), bg.reshape(M),
    )


def solution(mesh):
    in_specs = (P(None, ("row", "col"), None), P(), P(), P(), P(), P(), P("row", "col", None))
    out_specs = (P("row", "col", None), P(None, ("row", "col"), None), P(), P(), P(), P())
    return jax.shard_map(shards, mesh=mesh, in_specs=in_specs, out_specs=out_specs, check_vma=False)
```

```python
import functools

import jax
import jax.numpy as jnp
from jax import lax
from jax.experimental import pallas as pl
from jax.experimental.pallas import tpu as pltpu
from jax.sharding import PartitionSpec as P

F32, BF16 = jnp.float32, jnp.bfloat16
MESH = pl.DeviceIdType.MESH


def swap_blocks(parts, width):
    axis = parts[0].ndim - 1
    lane = lax.broadcasted_iota(jnp.int32, parts[0].shape, axis)
    a0, a1, a2, a3 = parts
    total = 4 * width
    half = lane < 2 * width
    t0 = jnp.where(half, a0, pltpu.roll(a2, 2 * width, axis))
    t2 = jnp.where(half, pltpu.roll(a0, 2 * width, axis), a2)
    t1 = jnp.where(half, a1, pltpu.roll(a3, 2 * width, axis))
    t3 = jnp.where(half, pltpu.roll(a1, 2 * width, axis), a3)
    even = lane % (2 * width) < width
    u0 = jnp.where(even, t0, pltpu.roll(t1, width, axis))
    u1 = jnp.where(even, pltpu.roll(t0, total - width, axis), t1)
    u2 = jnp.where(even, t2, pltpu.roll(t3, width, axis))
    u3 = jnp.where(even, pltpu.roll(t2, total - width, axis), t3)
    return [u0, u1, u2, u3]


def dot(a, b, ca, cb):
    return lax.dot_general(a, b, (((ca,), (cb,)), ((), ())), preferred_element_type=F32)


def kernel(
    cfg, x_hbm, gain_hbm, shift_hbm, map_hbm, w_hbm, bias_hbm, cot_hbm,
    pair_ref, align_ref, gout_ref, gxout_ref,
    gain_ref, shift_ref, map_ref, w_ref, bias_ref, cot_ref,
    xown, lbuf, rbuf, lf, cotf, pairf, glf, sl, sr, rl, rr, s1, r1, s2, r2, gbuf, ebuf, s1x, r1x, r2x, gx, pr, alignf, pairb, store,
    load, x_send, x_recv, e_send, e_recv, s1_send, s1_recv, s2_send, s2_recv,
    g2_send, g2_recv, g1_send, g1_recv, x1_send, x1_recv, x2_send, x2_recv, x3_send, x3_recv,
):
    R, C, BR, BC, S, M, K, CH1, EX, CH2, NO = cfg
    r, c = lax.axis_index("row"), lax.axis_index("col")
    n = r * C + c
    dest_col, dest_slot = lax.div(n, BC), lax.rem(n, BC)
    self_right = dest_col == c
    inv = 1.0 / S
    row_peers = [lax.rem(r + off, R) for off in range(1, R)]
    col_peers = [lax.rem(c + off, C) for off in range(1, C)]

    loads = [
        pltpu.make_async_copy(src, dst, load.at[i])
        for i, (src, dst) in enumerate([
            (x_hbm, xown), (cot_hbm, cot_ref), (w_hbm, w_ref), (map_hbm, map_ref),
            (gain_hbm, gain_ref), (shift_hbm, shift_ref), (bias_hbm, bias_ref),
        ])
    ]
    for cp in loads:
        cp.start()

    def other(rr_, cc_):
        return jnp.logical_or(rr_ != r, cc_ != c)

    owners = []
    for k in range(BC):
        o = c * BC + k
        owners.append((lax.div(o, C), lax.rem(o, C)))

    def signal(dev):
        pl.semaphore_signal(barrier, inc=1, device_id=dev, device_id_type=MESH)

    def remote(src, dst, send, recv, dev):
        return pltpu.make_async_remote_copy(
            src_ref=src, dst_ref=dst, send_sem=send, recv_sem=recv, device_id=dev, device_id_type=MESH
        )

    def owning(q, f):
        if NO == C:
            f()
        else:
            pl.when(q < NO)(f)

    barrier = pltpu.get_barrier_semaphore()
    for q in col_peers:
        signal((r, q))
    for p in row_peers:
        signal((p, c))
    for q in range(R):
        @pl.when(other(q, dest_col))
        def _():
            signal((q, dest_col))
    for k in range(BC):
        @pl.when(other(*owners[k]))
        def _():
            signal(owners[k])

    def standardized(x):
        mean = jnp.mean(x, axis=0, keepdims=True)
        cen = x - mean
        scale = lax.rsqrt(jnp.mean(cen * cen, axis=0, keepdims=True) + 1e-05)
        return cen * scale, scale

    early = (0, 3, 4, 5)
    for i in early:
        loads[i].wait()
    factor = jnp.transpose(jnp.broadcast_to(gain_ref[...], (S, M)))
    shift = jnp.transpose(jnp.broadcast_to(shift_ref[...], (S, M)))
    mapping = map_ref[...]
    mapping_t = jnp.transpose(mapping.astype(F32)).astype(BF16)
    own_unit, own_scale = standardized(xown[...].astype(F32))
    normed = (own_unit * factor + shift).astype(BF16)
    proj = dot(mapping_t, normed, 1, 0).astype(BF16)
    lbuf[c] = proj[:K]
    pr[...] = proj[K:]

    @pl.when(self_right)
    def _():
        rbuf[dest_slot] = proj[K:]

    pl.semaphore_wait(barrier, C - 1 + R - 1 + R + BC - jnp.where(self_right, 2, 0))

    pending = []

    def send(src, dst, ssem, rsem, dev, cond=None):
        cp = remote(src, dst, ssem, rsem, dev)
        if cond is None:
            cp.start()
        else:
            pl.when(cond)(cp.start)
        pending.append((cp, cond))

    for q in col_peers:
        send(lbuf.at[c], lbuf.at[c], x_send.at[q], x_recv.at[c], (r, q))
    for q in range(R):
        send(
            pr, rbuf.at[dest_slot], x_send.at[C + q], x_recv.at[BR + dest_slot],
            (q, dest_col), other(q, dest_col),
        )

    for i in range(len(loads)):
        if i not in early:
            loads[i].wait()
    cotf[...] = cot_ref[...].astype(F32)
    cot = jnp.concatenate([cotf[pl.ds(j, BR, stride=BC), :] for j in range(BC)], axis=0).astype(BF16)
    w = w_ref[...]
    groups = K * K // 128
    G = dot(cot, w, 1, 1).astype(BF16).astype(F32)
    tiles = []
    for t in range(BC // 4):
        parts = []
        for j in range(4):
            row = (4 * t + j) * BR
            parts.append(jnp.stack([G[row:row + BR, 128 * g:128 * g + 128] for g in range(groups)], axis=0))
        b = swap_blocks(parts, K)
        tiles.append(jnp.stack(b, axis=1).reshape(K * BR, 128))
    g2 = jnp.concatenate(tiles, axis=1).astype(BF16)

    for q in col_peers:
        remote(lbuf.at[q], lbuf.at[q], x_send.at[q], x_recv.at[q], (r, q)).wait_recv()
    for k in range(BC):
        @pl.when(other(*owners[k]))
        def _():
            remote(
                rbuf.at[k], rbuf.at[k], x_send.at[0], x_recv.at[BR + k], owners[k]
            ).wait_recv()

    for i in range(BR):
        lf[pl.ds(i, K, stride=BR), :] = lbuf[i].astype(F32)
    left = lf[...].astype(BF16)
    right = jnp.concatenate([rbuf[j] for j in range(BC)], axis=0)
    outer = (dot(left, right, 1, 1) * inv).astype(BF16).astype(F32)
    rows = []
    for t in range(BC // 4):
        o = outer[:, 128 * t:128 * t + 128].reshape(groups, 4, BR, 128)
        b = swap_blocks([o[:, q] for q in range(4)], K)
        for j in range(4):
            rows.append(jnp.concatenate([b[j][g] for g in range(groups)], axis=1))
    ot = jnp.concatenate(rows, axis=0).astype(BF16)

    wgrad = dot(ot, cot, 0, 0).astype(BF16)
    for p in range(R):
        s1[p] = wgrad[p * CH1:(p + 1) * CH1]
    for p in row_peers:
        send(s1.at[p], r1.at[r], s1_send.at[p], s1_recv.at[r], (p, c))

    glf[...] = dot(g2, right, 1, 0) * inv
    gr = (dot(g2, left, 0, 0) * inv).astype(BF16)
    for i in range(BR):
        gl = glf[pl.ds(i, K, stride=BR), :].astype(BF16)
        sl[i] = gl
    for j in range(BC):
        gg = gr[j * K:(j + 1) * K]
        sr[j] = gg
    rl[c] = sl[c]

    @pl.when(self_right)
    def _():
        rr[r] = sr[dest_slot]

    for q in col_peers:
        send(sl.at[q], rl.at[c], e_send.at[q], e_recv.at[c], (r, q))
    for k in range(BC):
        send(sr.at[k], rr.at[r], e_send.at[C + k], e_recv.at[C + r], owners[k], other(*owners[k]))

    def total(buf, count):
        acc = buf[0].astype(F32)
        for p in range(1, count):
            acc = acc + buf[p].astype(F32)
        return acc

    stores = []
    pairs = dot(ot, w, 1, 0) + bias_ref[...]
    for j in range(BC):
        pairf[pl.ds(j, BR, stride=BC), :] = pairs[j * BR:(j + 1) * BR]
    pairb[...] = pairf[...].astype(BF16)
    stores.append(pltpu.make_async_copy(pairb, pair_ref, store.at[1]))
    stores[-1].start()

    r1[r] = s1[r]
    for p in row_peers:
        remote(s1.at[p], r1.at[p], s1_send.at[p], s1_recv.at[p], (p, c)).wait_recv()
    s2[...] = total(r1, R).astype(BF16)

    def chunk(q):
        return pl.ds(pl.multiple_of(lax.rem(q, NO) * CH2, 16), CH2)

    for q in col_peers:
        send(s2.at[chunk(q)], r2.at[c], s2_send.at[q], s2_recv.at[c], (r, q))
    r2[c] = s2[chunk(c)]

    for q in col_peers:
        remote(sl.at[q], rl.at[q], e_send.at[q], e_recv.at[q], (r, q)).wait_recv()
    for q in range(R):
        @pl.when(other(q, dest_col))
        def _():
            remote(sr.at[0], rr.at[q], e_send.at[C], e_recv.at[C + q], (q, dest_col)).wait_recv()
    act = jnp.concatenate([total(rl, C), total(rr, R)], axis=0).astype(BF16)
    grad_normed = dot(mapping, act, 1, 0)
    ebuf[...] = jnp.zeros_like(ebuf)
    ebuf[:, :2 * K] = dot(normed, act, 1, 1)
    ebuf[:, 2 * K:2 * K + 1] = jnp.sum(grad_normed * own_unit, axis=1, keepdims=True)
    ebuf[:, 2 * K + 1:2 * K + 2] = jnp.sum(grad_normed, axis=1, keepdims=True)
    extra = ebuf[...].astype(BF16)
    for p in range(R):
        if p * EX < M:
            s1x[p] = extra[p * EX:(p + 1) * EX]
        else:
            s1x[p] = jnp.zeros((EX, 128), BF16)
    for p in row_peers:
        send(s1x.at[p], r1x.at[r], x1_send.at[p], x1_recv.at[r], (p, c))
    scaled = grad_normed * factor
    alignf[...] = own_scale * (
        scaled
        - jnp.mean(scaled, axis=0, keepdims=True)
        - own_unit * jnp.mean(scaled * own_unit, axis=0, keepdims=True)
    )

    stores.append(pltpu.make_async_copy(alignf, align_ref, store.at[0]))
    stores[-1].start()
    r1x[r] = s1x[r]
    for p in row_peers:
        remote(s1x.at[p], r1x.at[p], x1_send.at[p], x1_recv.at[p], (p, c)).wait_recv()
    r2x[c] = total(r1x, R).astype(BF16)
    for q in col_peers:
        send(r2x.at[c], r2x.at[c], x2_send.at[q], x2_recv.at[c], (r, q))

    for q in col_peers:
        remote(s2.at[chunk(q)], r2.at[q], s2_send.at[q], s2_recv.at[q], (r, q)).wait_recv()

    mine = chunk(c)
    result = total(r2, C).astype(BF16)

    half = NO // 2
    near = lax.div(lax.rem(c, NO), half)

    def group(h):
        return pl.ds(pl.multiple_of(h * half * CH2, 16), half * CH2)

    def forward(h, p):
        return remote(
            gbuf.at[r, group(h)], gout_ref.at[r, group(h)], g1_send.at[p * 2 + h], g1_recv.at[r * 2 + h], (p, c)
        )

    def spread():
        gbuf[r, mine, :] = result
        for q in col_peers:
            remote(gbuf.at[r, mine], gbuf.at[r, mine], g2_send.at[q], g2_recv.at[c], (r, q)).start()

    owning(c, spread)

    for q in col_peers:
        remote(r2x.at[q], r2x.at[q], x2_send.at[q], x2_recv.at[q], (r, q)).wait_recv()
    gx[r] = total(r2x, C).astype(BF16)
    for p in row_peers:
        send(gx.at[r], gxout_ref.at[r], x3_send.at[p], x3_recv.at[r], (p, c))
    stores.append(pltpu.make_async_copy(gx.at[r], gxout_ref.at[r], store.at[3]))
    stores[-1].start()

    for h in (near, 1 - near):
        for t in range(half):
            q = h * half + t

            @pl.when(q != c)
            def _():
                place = chunk(q)
                remote(gbuf.at[r, place], gbuf.at[r, place], g2_send.at[q], g2_recv.at[q], (r, q)).wait_recv()
        for p in row_peers:
            forward(h, p).start()
    stores.append(pltpu.make_async_copy(gbuf.at[r], gout_ref.at[r], store.at[2]))
    stores[-1].start()
    for p in row_peers:
        remote(gx.at[p], gxout_ref.at[p], x3_send.at[p], x3_recv.at[p], (p, c)).wait_recv()
        for h in range(2):
            remote(
                gbuf.at[p, group(h)], gout_ref.at[p, group(h)], g1_send.at[p * 2 + h], g1_recv.at[p * 2 + h], (p, c)
            ).wait_recv()
    for cp in stores:
        cp.wait()

    def spread_done():
        for q in col_peers:
            remote(gbuf.at[r, mine], gbuf.at[r, mine], g2_send.at[q], g2_recv.at[c], (r, q)).wait_send()

    owning(c, spread_done)
    for p in row_peers:
        for h in range(2):
            forward(h, p).wait_send()
    for cp, cond in pending:
        if cond is None:
            cp.wait_send()
        else:
            pl.when(cond)(cp.wait_send)


def finish(cfg, pair_in, align_in, g_in, gx_in, pair_ref, align_ref, proj_ref, wg_ref, gg_ref, bg_ref):
    R, K, M, EX, CH1 = cfg
    pair_ref[...] = pair_in[...]
    align_ref[...] = align_in[...]
    for p in range(R):
        wg_ref[p * CH1:(p + 1) * CH1, :] = g_in[p].astype(F32)
    e = jnp.concatenate([gx_in[p].astype(F32) for p in range(M // EX)], axis=0)
    proj_ref[...] = e[:, :2 * K]
    flipped = jnp.transpose(e)
    gg_ref[...] = flipped[2 * K:2 * K + 1, :]
    bg_ref[...] = flipped[2 * K + 1:2 * K + 2, :]


def shards(x, gain, shift, mapping, w, bias, cot):
    R, C = lax.axis_size("row"), lax.axis_size("col")
    S, M = x.shape[0], x.shape[2]
    K = mapping.shape[1] // 2
    BR, BC, E = cot.shape
    rows = w.shape[0]
    CH1, EX = rows // R, max(16, M // R)
    CH2 = max(16, CH1 // C)
    NO = CH1 // CH2
    cfg = (R, C, BR, BC, S, M, K, CH1, EX, CH2, NO)
    vm = pl.BlockSpec(memory_space=pltpu.VMEM)
    hbm = pl.BlockSpec(memory_space=pltpu.HBM)
    sem = pltpu.SemaphoreType.DMA
    shape = jax.ShapeDtypeStruct
    params = pltpu.CompilerParams(
        collective_id=0, has_side_effects=True, vmem_limit_bytes=58 * 1024 * 1024
    )
    parts = pl.pallas_call(
        functools.partial(kernel, cfg),
        out_shape=[
            shape((BR * BC, E), BF16), shape((M, S), F32),
            shape((R, CH1, E), BF16), shape((R, EX, E), BF16),
        ],
        in_specs=[hbm] * 7,
        out_specs=[hbm] * 4,
        scratch_shapes=[
            pltpu.VMEM((1, M), F32),
            pltpu.VMEM((1, M), F32),
            pltpu.VMEM(mapping.shape, BF16),
            pltpu.VMEM(w.shape, BF16),
            pltpu.VMEM((1, E), F32),
            pltpu.VMEM((BR * BC, E), BF16),
            pltpu.VMEM((M, S), BF16),
            pltpu.VMEM((BR, K, S), BF16),
            pltpu.VMEM((BC, K, S), BF16),
            pltpu.VMEM((K * BR, S), F32),
            pltpu.VMEM((BR * BC, E), F32),
            pltpu.VMEM((BR * BC, E), F32),
            pltpu.VMEM((K * BR, S), F32),
            pltpu.VMEM((BR, K, S), BF16),
            pltpu.VMEM((BC, K, S), BF16),
            pltpu.VMEM((C, K, S), BF16),
            pltpu.VMEM((R, K, S), BF16),
            pltpu.VMEM((R, CH1, E), BF16),
            pltpu.VMEM((R, CH1, E), BF16),
            pltpu.VMEM((CH1, E), BF16),
            pltpu.VMEM((C, CH2, E), BF16),
            pltpu.VMEM((R, CH1, E), BF16),
            pltpu.VMEM((M, E), F32),
            pltpu.VMEM((R, EX, E), BF16),
            pltpu.VMEM((R, EX, E), BF16),
            pltpu.VMEM((C, EX, E), BF16),
            pltpu.VMEM((R, EX, E), BF16),
            pltpu.VMEM((K, S), BF16),
            pltpu.VMEM((M, S), F32),
            pltpu.VMEM((BR * BC, E), BF16),
            sem((4,)),
            sem((7,)),
            sem((C + R,)), sem((BR + BC,)),
            sem((C + BC,)), sem((C + R,)),
            sem((R,)), sem((R,)),
            sem((C,)), sem((C,)),
            sem((C,)), sem((C,)),
            sem((R * 2,)), sem((R * 2,)),
            sem((R,)), sem((R,)),
            sem((C,)), sem((C,)),
            sem((R,)), sem((R,)),
        ],
        compiler_params=params,
        name="outer_mean",
    )(
        jnp.transpose(x, (1, 2, 0)).reshape(M, S), gain.reshape(1, M), shift.reshape(1, M), mapping, w,
        bias.reshape(1, E), cot.reshape(BR * BC, E),
    )
    pair, align, proj, wg, gg, bg = pl.pallas_call(
        functools.partial(finish, (R, K, M, EX, CH1)),
        out_shape=[
            shape((BR * BC, E), BF16), shape((M, S), F32), shape((M, 2 * K), F32),
            shape((rows, E), F32), shape((1, M), F32), shape((1, M), F32),
        ],
        in_specs=[vm] * 4,
        out_specs=[vm] * 6,
        compiler_params=pltpu.CompilerParams(vmem_limit_bytes=58 * 1024 * 1024),
        name="finish",
    )(*parts)
    return (
        pair.reshape(BR, BC, E), jnp.transpose(align.reshape(1, M, S), (2, 0, 1)), proj, wg,
        gg.reshape(M), bg.reshape(M),
    )


def solution(mesh):
    in_specs = (P(None, ("row", "col"), None), P(), P(), P(), P(), P(), P("row", "col", None))
    out_specs = (P("row", "col", None), P(None, ("row", "col"), None), P(), P(), P(), P())
    return jax.shard_map(shards, mesh=mesh, in_specs=in_specs, out_specs=out_specs, check_vma=False)
```
